128 devices in a mesh: strip: 4 (over x), tile: 32 (over z, y, core).
Axes of the slice: x: 4, y: 4, z: 4, core: 2. Of those that a mesh axis runs over, the one named last changes fastest.
Arguments:
- num_coef: bfloat16 [40, 65536], P(None, ('strip', 'tile')), may hold values from -1.25 to 1.25
- den_coef: bfloat16 [38, 65536], P(None, ('strip', 'tile')), may hold values from -0.039794922 to 0.039794922
- bias: float32 [6, 65536], P(None, ('strip', 'tile')), may hold values from -3 to 3
- scene_chain: int32 [65536], P(('strip', 'tile')), may hold values from 0 to 65535, as said below
- bucket_scenes: int32 [128, 1024], P(('strip', 'tile')), may hold values from 0 to 511
- tie_counts: int32 [128, 128], P(('strip', 'tile')), may hold values from 1 to 256, as said below
- tie_obs: float32 [2, 4194304], P(None, ('strip', 'tile')), may hold values from -1 to 1
- tie_prior: float32 [4194304], P(('strip', 'tile')), may hold values from 0.5 to 2
- tie_pick: int32 [4194304], P(('strip', 'tile')), may hold values from 0 to 7
- tie_point: int32 [4194304], P(('strip', 'tile')), may hold values from 0 to 2047
- ground: float32 [3, 262144], P(None, ('strip', 'tile')), may hold values from -1 to 1
Outputs:
- ground_next: float32 [3, 262144], P(None, ('strip', 'tile'))
- bias_step: float32 [6, 65536], P(None, ('strip', 'tile'))
The draws below stay inside these ranges and needn't reach their ends.
Inputs may be any that keep to these rules, and one draw needn't show every extreme that they name: The first tie_counts[d, e] of the 256 slots that device d holds for device e (its slots e * 256 to (e + 1) * 256 - 1) carry ties; the others are empty. `scene_chain`: each number appears once; strip s holds positions s * 16384 to (s + 1) * 16384 - 1 in along-track order. Scene j of the device with tile index t has its position in strip j // 128, within t * 512 to (t + 1) * 512 - 1 of that strip's positions. `bucket_scenes`: row d, entries e * 8 to (e + 1) * 8 - 1: local scenes of device d seen from the ground tiles of device e.
All inputs are finite; a program needn't handle non-finite values.
Results may differ from the reference program's by a relative error of at most 0.0003.
Values may be sent and summed in bfloat16 or wider, within the bound.
No kernel may reach another device: no remote copies, remote signals or barrier semaphores. Data moves between devices by JAX's collectives and lax.ppermute only.
A program may use at most 128 MiB of HBM per device.

```python
import math
import jax
import jax.numpy as jnp
from jax import lax

TIE_DEV = 32768
SC_DEV = 512
PTS_DEV = 2048
SCN_B = 8
SWEEPS = 4
STRIPS = 4
OWNERS = 128
CAP = 256
SCENES = 65536
STRIP_LEN = 16384
POINTS = 262144
TIES = 4194304
SCENE_SLOTS = 64


def draw_tie_counts(key, part):
    key = jax.random.fold_in(key, 11)
    key_light, key_heavy, key_forced = jax.random.split(key, 3)
    light = jax.random.randint(key_light, (OWNERS, OWNERS), 1, CAP // 2 + 1)
    heavy = jax.random.randint(key_heavy, (OWNERS,), 0, 4) == 0
    forced = jax.random.randint(key_forced, (), 0, OWNERS)
    heavy = heavy | (jnp.arange(OWNERS) == forced)
    return jnp.where(heavy[None, :], CAP, light).astype(jnp.int32)


def draw_scene_chain(key, part):
    key = jax.random.fold_in(key, 23)
    tiles_count = OWNERS // STRIPS
    per_strip = SC_DEV // STRIPS
    sub_keys = jax.random.split(key, OWNERS)
    slot_perm = jax.vmap(lambda sub_key: jax.random.permutation(sub_key, SC_DEV))(sub_keys)
    slot_perm = slot_perm.reshape(STRIPS, tiles_count, STRIPS, per_strip)
    offsets = (jnp.arange(STRIPS)[:, None] * tiles_count + jnp.arange(tiles_count)[None, :]) * SC_DEV
    placed = slot_perm + offsets[:, :, None, None]
    return jnp.transpose(placed, (2, 1, 0, 3)).reshape(SCENES).astype(jnp.int32)


def touch_ends(values, own_key, low, high):
    index_at = [jax.random.randint(jax.random.fold_in(own_key, axis), (), 0, length) for axis, length in enumerate(values.shape)]
    main_axis = values.shape.index(max(values.shape))
    beside = index_at[:main_axis] + [(index_at[main_axis] + 1) % values.shape[main_axis]] + index_at[main_axis + 1:]
    return values.at[tuple(index_at)].set(low).at[tuple(beside)].set(high)


def shard_levels(stream_key, extent, shards, least, high):
    gain = 1.0
    for dim, blocks in shards:
        draws = jax.random.uniform(jax.random.fold_in(jax.random.fold_in(stream_key, 6), dim), (blocks,), jnp.float32, least / len(shards), high / len(shards))
        gain = gain * jnp.repeat(jnp.exp(draws), extent[dim] // blocks).reshape((-1,) + (1,) * (len(extent) - 1 - dim))
    return gain


def noise(key, dims, width, most, shards=(), kind=jnp.bfloat16):
    drawn = width * jax.random.normal(key, dims, jnp.float32)
    if shards:
        drawn = drawn * shard_levels(key, dims, shards, -0.22, 0.18)
    return jnp.clip(drawn, -most, most).astype(kind)


def setup_inputs(seed: int = 0) -> dict:
    key_of = jax.random.split(jax.random.key(seed), 12)
    num_coef = noise(key_of[0], (40, SCENES), 20 ** -0.5, 1.25, ((1, 128),))
    den_coef = jnp.clip(jax.random.uniform(key_of[1], (38, SCENES), jnp.float32, -0.039794922, 0.039794922) * shard_levels(key_of[1], (38, SCENES), ((1, 128),), -0.4, 0.0), -0.039794922, 0.039794922).astype(jnp.bfloat16)
    bias = noise(key_of[2], (6, SCENES), 0.5, 3.0, ((1, 128),), jnp.float32)
    scene_chain = draw_scene_chain(jax.random.fold_in(key_of[11], 71), 0)
    bucket_scenes = touch_ends(jax.random.randint(key_of[4], (OWNERS, OWNERS * SCN_B), 0, SC_DEV), jax.random.fold_in(key_of[4], 1), 0, SC_DEV - 1).astype(jnp.int32)
    tie_counts = draw_tie_counts(jax.random.fold_in(key_of[11], 71), 0)
    tie_obs = jnp.clip(jax.random.uniform(key_of[6], (2, TIES), jnp.float32, -1.0, 1.0) * shard_levels(key_of[6], (2, TIES), ((1, 128),), -0.4, 0.0), -1.0, 1.0)
    tie_prior = jnp.clip(jnp.exp(math.log(2.0) - 1.3862944 * jax.random.uniform(key_of[7], (TIES,), jnp.float32) ** shard_levels(key_of[7], (TIES,), ((0, 128),), -0.2, 0.2)), 0.5, 2.0)
    tie_pick = touch_ends(jax.random.randint(key_of[8], (TIES,), 0, SCN_B), jax.random.fold_in(key_of[8], 1), 0, SCN_B - 1).astype(jnp.int32)
    tie_point = touch_ends(jax.random.randint(key_of[9], (TIES,), 0, PTS_DEV), jax.random.fold_in(key_of[9], 1), 0, PTS_DEV - 1).astype(jnp.int32)
    ground = jnp.clip(jax.random.uniform(key_of[10], (3, POINTS), jnp.float32, -1.0, 1.0) * shard_levels(key_of[10], (3, POINTS), ((1, 128),), -0.4, 0.0), -1.0, 1.0)
    return {"num_coef": num_coef, "den_coef": den_coef, "bias": bias, "scene_chain": scene_chain, "bucket_scenes": bucket_scenes, "tie_counts": tie_counts, "tie_obs": tie_obs, "tie_prior": tie_prior, "tie_pick": tie_pick, "tie_point": tie_point, "ground": ground}


cauchy_scale = 1.0
point_damping = 1.0
smooth_gain = 0.25


def monomial_tables(ground_pos):
    east_x = ground_pos[0]
    north_y = ground_pos[1]
    up_z = ground_pos[2]
    zero_row = jnp.zeros_like(east_x)
    ones_row = jnp.ones_like(east_x)
    east_sq = east_x * east_x
    north_sq = north_y * north_y
    up_sq = up_z * up_z
    values = jnp.stack([ones_row, east_x, north_y, up_z, east_x * north_y, east_x * up_z, north_y * up_z, east_sq, north_sq, up_sq, north_y * east_x * up_z, east_sq * east_x, east_x * north_sq, east_x * up_sq, east_sq * north_y, north_sq * north_y, north_y * up_sq, east_sq * up_z, north_sq * up_z, up_sq * up_z])
    by_east = jnp.stack([zero_row, ones_row, zero_row, zero_row, north_y, up_z, zero_row, 2.0 * east_x, zero_row, zero_row, north_y * up_z, 3.0 * east_sq, north_sq, up_sq, 2.0 * east_x * north_y, zero_row, zero_row, 2.0 * east_x * up_z, zero_row, zero_row])
    by_north = jnp.stack([zero_row, zero_row, ones_row, zero_row, east_x, zero_row, up_z, zero_row, 2.0 * north_y, zero_row, east_x * up_z, zero_row, 2.0 * east_x * north_y, zero_row, east_sq, 3.0 * north_sq, up_sq, zero_row, 2.0 * north_y * up_z, zero_row])
    by_up = jnp.stack([zero_row, zero_row, zero_row, ones_row, zero_row, east_x, north_y, zero_row, zero_row, 2.0 * up_z, north_y * east_x, zero_row, zero_row, 2.0 * east_x * up_z, zero_row, zero_row, 2.0 * north_y * up_z, east_sq, north_sq, 3.0 * up_sq])
    return values, (by_east, by_north, by_up)


def rational(numer, denom, values, slopes):
    numerator = jnp.sum(numer * values, axis=0)
    bottom = 1.0 + jnp.sum(denom * values[1:], axis=0)
    quotient = numerator / bottom
    partials = [(jnp.sum(numer * slope_table, axis=0) - quotient * jnp.sum(denom * slope_table[1:], axis=0)) / bottom for slope_table in slopes]
    return quotient, partials


def project_ties(tie_coefs, bias_rows, obs_rows, ground_pos):
    values, slopes = monomial_tables(ground_pos)
    line_ratio, line_partials = rational(tie_coefs[0:20], tie_coefs[40:59], values, slopes)
    samp_ratio, samp_partials = rational(tie_coefs[20:40], tie_coefs[59:78], values, slopes)
    line_obs = obs_rows[0]
    sample_obs = obs_rows[1]
    line_res = line_obs - (line_ratio + bias_rows[0] + bias_rows[1] * sample_obs + bias_rows[2] * line_obs)
    samp_res = sample_obs - (samp_ratio + bias_rows[3] + bias_rows[4] * sample_obs + bias_rows[5] * line_obs)
    return jnp.stack([line_res, samp_res] + line_partials + samp_partials)


def point_terms(packed, prior_live):
    line_res = packed[0]
    samp_res = packed[1]
    weight = prior_live / (1.0 + (line_res * line_res + samp_res * samp_res) / cauchy_scale)
    line_jac = packed[2:5]
    samp_jac = packed[5:8]
    upper_pairs = [(0, 0), (0, 1), (0, 2), (1, 1), (1, 2), (2, 2)]
    point_rows = [weight * (line_jac[row_a] * line_jac[row_b] + samp_jac[row_a] * samp_jac[row_b]) for row_a, row_b in upper_pairs]
    point_rows = point_rows + [weight * (line_jac[row_a] * line_res + samp_jac[row_a] * samp_res) for row_a in range(3)]
    return weight, jnp.stack(point_rows)


def inverse_sym(matrix):
    cofactor = [matrix[3] * matrix[5] - matrix[4] * matrix[4], matrix[2] * matrix[4] - matrix[1] * matrix[5], matrix[1] * matrix[4] - matrix[2] * matrix[3], matrix[0] * matrix[5] - matrix[2] * matrix[2], matrix[1] * matrix[2] - matrix[0] * matrix[4], matrix[0] * matrix[3] - matrix[1] * matrix[1]]
    determinant = matrix[0] * cofactor[0] + matrix[1] * cofactor[1] + matrix[2] * cofactor[2]
    return [cofactor_entry / determinant for cofactor_entry in cofactor]


def apply_sym(inverse, comp_one, comp_two, comp_three):
    return [inverse[0] * comp_one + inverse[1] * comp_two + inverse[2] * comp_three, inverse[1] * comp_one + inverse[3] * comp_two + inverse[4] * comp_three, inverse[2] * comp_one + inverse[4] * comp_two + inverse[5] * comp_three]


def solve_points(point_sums):
    matrix = [point_sums[0] + point_damping, point_sums[1], point_sums[2], point_sums[3] + point_damping, point_sums[4], point_sums[5] + point_damping]
    return jnp.stack(apply_sym(inverse_sym(matrix), point_sums[6], point_sums[7], point_sums[8]))


def scene_terms(packed, weight, obs_rows, tie_step):
    line_res = packed[0] - (packed[2] * tie_step[0] + packed[3] * tie_step[1] + packed[4] * tie_step[2])
    samp_res = packed[1] - (packed[5] * tie_step[0] + packed[6] * tie_step[1] + packed[7] * tie_step[2])
    line_obs = obs_rows[0]
    sample_obs = obs_rows[1]
    samp_weight = weight * sample_obs
    line_weight = weight * line_obs
    return jnp.stack([weight, samp_weight, line_weight, samp_weight * sample_obs, samp_weight * line_obs, line_weight * line_obs, weight * line_res, samp_weight * line_res, line_weight * line_res, weight * samp_res, samp_weight * samp_res, line_weight * samp_res])


def chain_inverse(normal_sums, coupling):
    matrix = [normal_sums[0] + 2.0 * coupling, normal_sums[1], normal_sums[2], normal_sums[3] + 2.0 * coupling, normal_sums[4], normal_sums[5] + 2.0 * coupling]
    return inverse_sym(matrix)


def apply_pair(inverse, vectors):
    return jnp.stack(apply_sym(inverse, vectors[0], vectors[1], vectors[2]) + apply_sym(inverse, vectors[3], vectors[4], vectors[5]))


def reference(num_coef, den_coef, bias, scene_chain, bucket_scenes, tie_counts, tie_obs, tie_prior, tie_pick, tie_point, ground):
    coef_table = jnp.concatenate([num_coef, den_coef], axis=0)
    slot_ids = jnp.arange(TIE_DEV, dtype=jnp.int32)
    target = slot_ids // CAP
    in_bucket = slot_ids % CAP

    def per_owner(owner_id):
        row_start = (owner_id * TIE_DEV).astype(jnp.int32)
        counts_row = lax.dynamic_index_in_dim(tie_counts, owner_id, 0, keepdims=False)
        live_mask = (in_bucket < jnp.take(counts_row, target)).astype(jnp.float32)
        scene_lists = lax.dynamic_index_in_dim(bucket_scenes, owner_id, 0, keepdims=False)
        tie_picks = lax.dynamic_slice_in_dim(tie_pick, row_start, TIE_DEV)
        local_scene = jnp.take(scene_lists, target * SCN_B + tie_picks)
        scene_ids = (owner_id * SC_DEV + local_scene).astype(jnp.int32)
        point_ids = (target * PTS_DEV + lax.dynamic_slice_in_dim(tie_point, row_start, TIE_DEV)).astype(jnp.int32)
        obs_rows = lax.dynamic_slice_in_dim(tie_obs, row_start, TIE_DEV, 1)
        prior_live = lax.dynamic_slice_in_dim(tie_prior, row_start, TIE_DEV) * live_mask
        tie_coefs = jnp.take(coef_table, scene_ids, axis=1).astype(jnp.float32)
        packed = project_ties(tie_coefs, jnp.take(bias, scene_ids, axis=1), obs_rows, jnp.take(ground, point_ids, axis=1))
        return packed, prior_live, point_ids, jnp.take(scene_chain, scene_ids)

    packed, prior_live, point_ids, chain_ids = lax.map(per_owner, jnp.arange(OWNERS, dtype=jnp.int32))
    packed = jnp.moveaxis(packed, 0, 1).reshape(8, TIES)
    prior_live = prior_live.reshape(TIES)
    point_ids = point_ids.reshape(TIES)
    chain_ids = chain_ids.reshape(TIES)
    weight, point_rows = point_terms(packed, prior_live)
    point_sums = jnp.zeros((9, POINTS), jnp.float32).at[:, point_ids].add(point_rows)
    point_step = solve_points(point_sums)
    ground_next = ground + point_step
    scene_rows = scene_terms(packed, weight, tie_obs, jnp.take(point_step, point_ids, axis=1))
    normal_sums = jnp.zeros((12, SCENES), jnp.float32).at[:, chain_ids].add(scene_rows)
    normal_sums = normal_sums.reshape(12, STRIPS, STRIP_LEN)
    coupling = smooth_gain * SCENE_SLOTS
    inverse = chain_inverse(normal_sums, coupling)
    rhs_rows = normal_sums[6:12]
    smoothed = apply_pair(inverse, rhs_rows)
    for sweep_idx in range(SWEEPS - 1):
        padded = jnp.pad(smoothed, ((0, 0), (0, 0), (1, 1)))
        smoothed = apply_pair(inverse, rhs_rows + coupling * (padded[:, :, :-2] + padded[:, :, 2:]))
    return ground_next, smoothed.reshape(6, SCENES)
```

```python
import functools

import jax
import jax.numpy as jnp
from jax import lax
from jax.experimental import pallas as pl
from jax.experimental.pallas import tpu as pltpu
from jax.sharding import PartitionSpec as P

SWEEPS = 4
AXES = ("strip", "tile")
F32 = jnp.float32
BF16 = jnp.bfloat16
I32 = jnp.int32
LANES = 128
SUB = 8

cauchy_scale = 1.0
point_damping = 1.0
smooth_gain = 0.25

NUM_ROW = 0
DEN_ROW = 40
BIAS_ROW = 80
BIAS_SPLIT = 8
CHAIN_ROW = 104
SCENE_LANES = 16
POS_LANE = 12


def lane_iota(shape):
    return lax.broadcasted_iota(I32, shape, len(shape) - 1)


def sublane_iota(shape):
    return lax.broadcasted_iota(I32, shape, len(shape) - 2)


def split3(value):
    high = value.astype(BF16).astype(F32)
    rest = value - high
    middle = rest.astype(BF16).astype(F32)
    return high, middle, rest - middle


def gather_lanes(row, lanes):
    table = jnp.broadcast_to(row, lanes.shape)
    return jnp.take_along_axis(table, lanes, axis=1, mode="promise_in_bounds")


def inverse_sym(matrix):
    cofactor = [
        matrix[3] * matrix[5] - matrix[4] * matrix[4],
        matrix[2] * matrix[4] - matrix[1] * matrix[5],
        matrix[1] * matrix[4] - matrix[2] * matrix[3],
        matrix[0] * matrix[5] - matrix[2] * matrix[2],
        matrix[1] * matrix[2] - matrix[0] * matrix[4],
        matrix[0] * matrix[3] - matrix[1] * matrix[1],
    ]
    determinant = matrix[0] * cofactor[0] + matrix[1] * cofactor[1] + matrix[2] * cofactor[2]
    return [cofactor_entry / determinant for cofactor_entry in cofactor]


def apply_sym(inverse, comp_one, comp_two, comp_three):
    return [
        inverse[0] * comp_one + inverse[1] * comp_two + inverse[2] * comp_three,
        inverse[1] * comp_one + inverse[3] * comp_two + inverse[4] * comp_three,
        inverse[2] * comp_one + inverse[4] * comp_two + inverse[5] * comp_three,
    ]


def ties_kernel(obs_ref, prior_ref, pick_ref, point_ref, counts_ref, out_ref):
    owners = out_ref.shape[0] // 8
    counts = jnp.broadcast_to(counts_ref[...].astype(F32), (owners, owners)).T
    slot = lane_iota((SUB, LANES)).astype(F32)
    for group in range(owners // SUB):
        live_count = counts[group * SUB : (group + 1) * SUB, :1]
        base = group * SUB * 8
        for row in range(4):
            out_ref[pl.ds(base + row, SUB, stride=8), :] = obs_ref[
                pl.ds(group * SUB * 4 + row, SUB, stride=4), :
            ]
        for half in range(2):
            rows = pl.ds(group * SUB * 2 + half, SUB, stride=2)
            live = slot + float(half * LANES) < live_count
            out_ref[pl.ds(base + 4 + half, SUB, stride=8), :] = jnp.where(
                live, prior_ref[rows, :], 0.0
            )
            out_ref[pl.ds(base + 6 + half, SUB, stride=8), :] = (
                pick_ref[rows, :] * 2048 + point_ref[rows, :]
            ).astype(F32)


def scenes_kernel(num_ref, den_ref, bias_ref, chain_ref, list_ref, out_ref, table_ref):
    scenes = num_ref.shape[1]
    listed = list_ref.shape[1]
    table_ref[...] = jnp.zeros(table_ref.shape, F32)
    table_ref[NUM_ROW : NUM_ROW + 40, :] = num_ref[...].astype(F32)
    table_ref[DEN_ROW : DEN_ROW + 38, :] = den_ref[...].astype(F32)
    for part, value in enumerate(split3(bias_ref[...])):
        first = BIAS_ROW + part * BIAS_SPLIT
        table_ref[first : first + 6, :] = value
    place = (chain_ref[...] & (scenes - 1)) + (lane_iota((1, scenes)) // (scenes // 4)) * scenes
    table_ref[CHAIN_ROW : CHAIN_ROW + 1, :] = (place >> 8).astype(F32)
    table_ref[CHAIN_ROW + 1 : CHAIN_ROW + 2, :] = (place & 255).astype(F32)
    table = table_ref[...].astype(BF16)
    for first in range(0, listed, 256):
        chosen = jnp.broadcast_to(list_ref[:, first : first + 256], (scenes, 256))
        onehot = jnp.where(chosen == sublane_iota((scenes, 256)), 1.0, 0.0).astype(BF16)
        got = jnp.dot(table, onehot, preferred_element_type=F32)
        for part in range(0, 256, LANES):
            out_ref[first + part : first + part + LANES, :] = got[:, part : part + LANES].T.astype(
                out_ref.dtype
            )


def rational(coef, numer, denom, east, north, up):
    east_sq, north_sq, up_sq = east * east, north * north, up * up
    east_north, east_up, north_up = east * north, east * up, north * up
    terms = [
        (None, None, None, None),
        (east, 1, None, None),
        (north, None, 1, None),
        (up, None, None, 1),
        (east_north, north, east, None),
        (east_up, up, None, east),
        (north_up, None, up, north),
        (east_sq, 2.0 * east, None, None),
        (north_sq, None, 2.0 * north, None),
        (up_sq, None, None, 2.0 * up),
        (east_north * up, north_up, east_up, east_north),
        (east_sq * east, 3.0 * east_sq, None, None),
        (east * north_sq, north_sq, 2.0 * east_north, None),
        (east * up_sq, up_sq, None, 2.0 * east_up),
        (east_sq * north, 2.0 * east_north, east_sq, None),
        (north_sq * north, None, 3.0 * north_sq, None),
        (north * up_sq, None, up_sq, 2.0 * north_up),
        (east_sq * up, 2.0 * east_up, None, east_sq),
        (north_sq * up, None, 2.0 * north_up, north_sq),
        (up_sq * up, None, None, 3.0 * up_sq),
    ]

    def cubic(first, start):
        sums = [start, None, None, None]
        for index, factors in enumerate(terms):
            if index == 0:
                if start is None:
                    sums[0] = coef(first)
                    first = first + 1
                continue
            value = coef(first + index - 1)
            for which, factor in enumerate(factors):
                if factor is None:
                    continue
                product = value if isinstance(factor, int) else value * factor
                sums[which] = product if sums[which] is None else sums[which] + product
        return sums

    top = cubic(numer, None)
    bottom = cubic(denom, jnp.ones_like(east))
    quotient = top[0] / bottom[0]
    partials = [
        (top[which] - quotient * bottom[which]) / bottom[0] for which in range(1, 4)
    ]
    return quotient, partials


def tile_kernel(
    ties_ref,
    scenes_ref,
    ground_ref,
    next_ref,
    out_ref,
    coef_ref,
    packed_ref,
    parts_ref,
    index_ref,
    sums_ref,
    step_ref,
    *,
    strips,
):
    owners = ties_ref.shape[0] // 8
    groups = owners // SUB
    points = ground_ref.shape[1]
    point_rows = points // LANES
    vreg = (SUB, LANES)

    for block in range(owners * 8 // LANES):
        rows = slice(block * LANES, (block + 1) * LANES)
        turned = scenes_ref[rows, :].astype(F32).T
        bias_rows = (
            turned[BIAS_ROW : BIAS_ROW + 8]
            + turned[BIAS_ROW + 8 : BIAS_ROW + 16]
            + turned[BIAS_ROW + 16 : BIAS_ROW + 24]
        )
        coef_ref[rows, :] = turned
        coef_ref[block * LANES + BIAS_ROW : block * LANES + BIAS_ROW + 8, :] = bias_rows

    def tie_row(group, row):
        return ties_ref[pl.ds(group * SUB * 8 + row, SUB, stride=8), :]

    def code_of(group, half):
        code = tie_row(group, 6 + half).astype(I32)
        return code >> 11, code & (points - 1)

    def gather_points(table, point):
        high = point >> 7
        low = point & (LANES - 1)
        found = [jnp.zeros(vreg, F32)] * 3
        for row in range(point_rows):
            here = high == row
            for axis in range(3):
                found[axis] = jnp.where(here, gather_lanes(table(axis, row), low), found[axis])
        return found

    def first_pass(group, carry):
        base = (group // 2) * LANES
        for half in range(2):
            pick, point = code_of(group, half)
            lanes = ((group % 2) * SUB + sublane_iota(vreg)) * 8 + pick
            east, north, up = gather_points(
                lambda axis, row: ground_ref[axis : axis + 1, row * LANES : (row + 1) * LANES],
                point,
            )

            def coef(row):
                return gather_lanes(coef_ref[pl.ds(base + row, 1), :], lanes)

            line_obs = tie_row(group, 2 * half)
            samp_obs = tie_row(group, 2 * half + 1)
            prior = tie_row(group, 4 + half)
            line_ratio, line_jac = rational(coef, NUM_ROW, DEN_ROW, east, north, up)
            samp_ratio, samp_jac = rational(coef, NUM_ROW + 20, DEN_ROW + 19, east, north, up)
            line_res = line_obs - (
                line_ratio
                + coef(BIAS_ROW)
                + coef(BIAS_ROW + 1) * samp_obs
                + coef(BIAS_ROW + 2) * line_obs
            )
            samp_res = samp_obs - (
                samp_ratio
                + coef(BIAS_ROW + 3)
                + coef(BIAS_ROW + 4) * samp_obs
                + coef(BIAS_ROW + 5) * line_obs
            )
            weight = prior / (1.0 + (line_res * line_res + samp_res * samp_res) / cauchy_scale)
            place = pl.ds((group * 2 + half) * SUB, SUB)
            for row, value in enumerate([line_res, samp_res] + line_jac + samp_jac + [weight]):
                packed_ref[row, place, :] = value
            pairs = [(0, 0), (0, 1), (0, 2), (1, 1), (1, 2), (2, 2)]
            sums = [
                weight * (line_jac[a] * line_jac[b] + samp_jac[a] * samp_jac[b]) for a, b in pairs
            ]
            sums += [weight * (line_jac[a] * line_res + samp_jac[a] * samp_res) for a in range(3)]
            for row, value in enumerate(sums):
                for part, piece in enumerate(split3(value)):
                    parts_ref[row * 3 + part, place, :] = piece
            index_ref[0, place, :] = point >> 8
            index_ref[1, place, :] = point & 255
        return carry

    lax.fori_loop(0, groups, first_pass, 0)

    sums_ref[...] = jnp.zeros(sums_ref.shape, F32)
    per_step = 4

    def sum_pass(step, carry):
        left = []
        right = []
        for bucket in range(per_step):
            index = step * per_step + bucket
            for half in range(2):
                row = ((index // SUB) * 2 + half) * SUB + index % SUB
                mask = jnp.broadcast_to(index_ref[0, pl.ds(row, 1), :], vreg) == sublane_iota(vreg)
                columns = [
                    jnp.where(mask, jnp.broadcast_to(parts_ref[part, pl.ds(row, 1), :], vreg), 0.0)
                    for part in range(27)
                ]
                columns.append(jnp.zeros(vreg, F32))
                left.append(jnp.concatenate(columns, axis=0).astype(BF16))
                low = jnp.broadcast_to(index_ref[1, pl.ds(row, 1), :], (256, LANES))
                right.append(
                    jnp.where(low == sublane_iota((256, LANES)), 1.0, 0.0).astype(BF16)
                )
        sums_ref[...] += lax.dot_general(
            jnp.concatenate(left, axis=1),
            jnp.concatenate(right, axis=1),
            (((1,), (1,)), ((), ())),
            preferred_element_type=F32,
        )
        return carry

    lax.fori_loop(0, owners // per_step, sum_pass, 0)

    def point_sum(row):
        first = row * 3 * SUB
        return (
            sums_ref[first : first + SUB, :]
            + sums_ref[first + SUB : first + 2 * SUB, :]
            + sums_ref[first + 2 * SUB : first + 3 * SUB, :]
        )

    sums = [point_sum(row) for row in range(9)]
    matrix = [
        sums[0] + point_damping,
        sums[1],
        sums[2],
        sums[3] + point_damping,
        sums[4],
        sums[5] + point_damping,
    ]
    steps = apply_sym(inverse_sym(matrix), sums[6], sums[7], sums[8])
    for axis in range(3):
        for half in range(2):
            step_ref[pl.ds(axis * point_rows + half, SUB, stride=2), :] = steps[axis][
                :, half * LANES : (half + 1) * LANES
            ]
        for row in range(point_rows):
            columns = slice(row * LANES, (row + 1) * LANES)
            at = axis * point_rows + row
            next_ref[axis : axis + 1, columns] = (
                ground_ref[axis : axis + 1, columns] + step_ref[at : at + 1, :]
            )

    def second_pass(group, carry):
        rows = []
        picks = []
        for half in range(2):
            pick, point = code_of(group, half)
            tie_step = gather_points(
                lambda axis, row: step_ref[axis * point_rows + row : axis * point_rows + row + 1, :],
                point,
            )
            place = pl.ds((group * 2 + half) * SUB, SUB)
            packed = [packed_ref[row, place, :] for row in range(9)]
            line_obs = tie_row(group, 2 * half)
            samp_obs = tie_row(group, 2 * half + 1)
            weight = packed[8]
            line_res = packed[0] - (
                packed[2] * tie_step[0] + packed[3] * tie_step[1] + packed[4] * tie_step[2]
            )
            samp_res = packed[1] - (
                packed[5] * tie_step[0] + packed[6] * tie_step[1] + packed[7] * tie_step[2]
            )
            samp_weight = weight * samp_obs
            line_weight = weight * line_obs
            rows.append(
                [
                    weight,
                    samp_weight,
                    line_weight,
                    samp_weight * samp_obs,
                    samp_weight * line_obs,
                    line_weight * line_obs,
                    weight * line_res,
                    samp_weight * line_res,
                    line_weight * line_res,
                    weight * samp_res,
                    samp_weight * samp_res,
                    line_weight * samp_res,
                ]
            )
            picks.append(pick)
        lane = lane_iota(vreg)
        total = jnp.zeros(vreg, F32)
        for scene in range(8):
            first, second = picks[0] == scene, picks[1] == scene
            for row in range(12):
                both = jnp.where(first, rows[0][row], 0.0) + jnp.where(second, rows[1][row], 0.0)
                total = jnp.where(
                    lane == scene * SCENE_LANES + row,
                    jnp.sum(both, axis=1, keepdims=True),
                    total,
                )
        base = (group // 2) * LANES
        lanes = ((group % 2) * SUB + sublane_iota(vreg)) * 8 + lane // SCENE_LANES
        high = gather_lanes(coef_ref[pl.ds(base + CHAIN_ROW, 1), :], lanes)
        low = gather_lanes(coef_ref[pl.ds(base + CHAIN_ROW + 1, 1), :], lanes)
        place = high * 256.0 + low
        tiles = owners // strips
        source = group // (tiles // SUB)
        tile = (group % (tiles // SUB)) * SUB
        for strip in range(strips):
            start = float(strip * 4 * LANES)
            inside = (place >= start) & (place < start + 4 * LANES)
            position = jnp.where(inside, place - start, -1.0)
            out_ref[pl.ds((strip * tiles + tile) * strips + source, SUB, stride=strips), :] = (
                jnp.where(lane % SCENE_LANES == POS_LANE, position, total)
            )
        return carry

    lax.fori_loop(0, groups, second_pass, 0)


def segment_kernel(got_ref, sums_ref, low_ref, high_ref):
    scenes = sums_ref.shape[1]
    total = jnp.zeros((3 * SCENE_LANES, scenes), F32)
    for first in range(0, got_ref.shape[0], LANES):
        turned = got_ref[first : first + LANES, :].T
        values = jnp.concatenate(
            [turned[k * SCENE_LANES : (k + 1) * SCENE_LANES] for k in range(8)], axis=1
        )
        position = values[POS_LANE : POS_LANE + 1].astype(I32)
        onehot = jnp.where(
            jnp.broadcast_to(position, (scenes, 8 * LANES)) == sublane_iota((scenes, 8 * LANES)),
            1.0,
            0.0,
        ).astype(BF16)
        pieces = jnp.concatenate(split3(values), axis=0).astype(BF16)
        total = total + lax.dot_general(
            pieces, onehot, (((1,), (1,)), ((), ())), preferred_element_type=F32
        )
    sums = total[:16] + total[16:32] + total[32:48]
    sums = jnp.where(sublane_iota(sums.shape) == POS_LANE, 1.0, sums)
    sums_ref[...] = sums
    low_ref[...] = sums[:, :LANES]
    high_ref[...] = sums[:, scenes - LANES :]


def chain_kernel(left_ref, sums_ref, right_ref, out_ref, *, coupling):
    scenes = sums_ref.shape[1]
    sums = jnp.concatenate([left_ref[...], sums_ref[...], right_ref[...]], axis=1)
    width = sums.shape[1]
    rows = [sums[row : row + 1] for row in range(13)]
    matrix = [
        rows[0] + 2.0 * coupling,
        rows[1],
        rows[2],
        rows[3] + 2.0 * coupling,
        rows[4],
        rows[5] + 2.0 * coupling,
    ]
    inverse = [entry * rows[POS_LANE] for entry in inverse_sym(matrix)]

    def apply_pair(vectors):
        return apply_sym(inverse, *vectors[:3]) + apply_sym(inverse, *vectors[3:])

    right_sides = rows[6:12]
    smoothed = apply_pair(right_sides)
    for _ in range(SWEEPS - 1):
        smoothed = apply_pair(
            [
                side + coupling * (pltpu.roll(value, 1, 1) + pltpu.roll(value, width - 1, 1))
                for side, value in zip(right_sides, smoothed)
            ]
        )
    for row in range(6):
        out_ref[row : row + 1, :] = smoothed[row][:, LANES : LANES + scenes]


def call(kernel, out_shape, scratch=(), name=None):
    return pl.pallas_call(
        kernel,
        out_shape=out_shape,
        scratch_shapes=list(scratch),
        compiler_params=pltpu.CompilerParams(vmem_limit_bytes=48 * 1024 * 1024),
        name=name,
    )


def shape(dims, dtype=F32):
    return jax.ShapeDtypeStruct(dims, dtype)


def per_device(
    num_coef,
    den_coef,
    bias,
    scene_chain,
    bucket_scenes,
    tie_counts,
    tie_obs,
    tie_prior,
    tie_pick,
    tie_point,
    ground,
):
    strips = lax.axis_size("strip")
    tiles = lax.axis_size("tile")
    owners = strips * tiles
    tie_dev = tie_prior.shape[0]
    tie_rows = tie_dev // LANES
    scenes_dev = num_coef.shape[1]
    listed = bucket_scenes.shape[1]
    points_dev = ground.shape[1]
    coupling = smooth_gain * (tie_dev // scenes_dev)

    obs = tie_obs.reshape(2, tie_rows, LANES).transpose(1, 0, 2).reshape(2 * tie_rows, LANES)
    ties = call(ties_kernel, shape((owners * 8, LANES)), name="pack_ties")(
        obs,
        tie_prior.reshape(tie_rows, LANES),
        tie_pick.reshape(tie_rows, LANES),
        tie_point.reshape(tie_rows, LANES),
        tie_counts,
    )
    got_ties = lax.all_to_all(ties.reshape(owners, 8, LANES), AXES, 0, 0, tiled=True)
    scenes = call(
        scenes_kernel,
        shape((listed, LANES), BF16),
        [pltpu.VMEM((LANES, scenes_dev), F32)],
        name="pack_scenes",
    )(num_coef, den_coef, bias, scene_chain.reshape(1, scenes_dev), bucket_scenes)
    got_scenes = lax.all_to_all(scenes.reshape(owners, 8, LANES), AXES, 0, 0, tiled=True)
    ground_next, totals = call(
        functools.partial(tile_kernel, strips=strips),
        (shape((3, points_dev)), shape((owners * strips, LANES))),
        [
            pltpu.VMEM((owners * 8, LANES), F32),
            pltpu.VMEM((9, tie_rows, LANES), F32),
            pltpu.VMEM((27, tie_rows, LANES), F32),
            pltpu.VMEM((2, tie_rows, LANES), I32),
            pltpu.VMEM((28 * SUB, 256), F32),
            pltpu.VMEM((3 * points_dev // LANES, LANES), F32),
        ],
        name="tile_sums",
    )(got_ties.reshape(owners * 8, LANES), got_scenes.reshape(listed, LANES), ground)
    got_totals = lax.all_to_all(totals.reshape(owners, strips, LANES), AXES, 0, 0, tiled=True)
    sums, low, high = call(
        segment_kernel,
        (shape((16, scenes_dev)), shape((16, LANES)), shape((16, LANES))),
        name="segment_sums",
    )(got_totals.reshape(owners * strips, LANES))
    forward = [(i, i + 1) for i in range(tiles - 1)]
    backward = [(target, source) for source, target in forward]
    left = lax.ppermute(high, "tile", forward)
    right = lax.ppermute(low, "tile", backward)
    smoothed = call(
        functools.partial(chain_kernel, coupling=coupling),
        shape((6, scenes_dev)),
        name="chain",
    )(left, sums, right)
    return ground_next, smoothed


def solution(mesh):
    in_specs = (
        P(None, AXES),
        P(None, AXES),
        P(None, AXES),
        P(AXES),
        P(AXES, None),
        P(AXES, None),
        P(None, AXES),
        P(AXES),
        P(AXES),
        P(AXES),
        P(None, AXES),
    )
    out_specs = (P(None, AXES), P(None, AXES))
    return jax.shard_map(
        per_device, mesh=mesh, in_specs=in_specs, out_specs=out_specs, check_vma=False
    )
```

```python
import functools

import jax
import jax.numpy as jnp
from jax import lax
from jax.experimental import pallas as pl
from jax.experimental.pallas import tpu as pltpu
from jax.sharding import PartitionSpec as P

SWEEPS = 4
AXES = ("strip", "tile")
F32 = jnp.float32
BF16 = jnp.bfloat16
I32 = jnp.int32
LANES = 128
SUB = 8

cauchy_scale = 1.0
point_damping = 1.0
smooth_gain = 0.25

LATE_TERMS = 64
BIAS_ROW = 80
CHAIN_ROW = 104
CHAIN_SENT = 88
SCENE_ROWS = 6
BUCKET_ROWS = 8 + SCENE_ROWS
SCENE_LANES = 16
POS_LANE = 12
HALO = SWEEPS - 1
PART_ROWS = 32


def lane_iota(shape):
    return lax.broadcasted_iota(I32, shape, len(shape) - 1)


def sublane_iota(shape):
    return lax.broadcasted_iota(I32, shape, len(shape) - 2)


def split3(value):
    high = value.astype(BF16).astype(F32)
    rest = value - high
    middle = rest.astype(BF16).astype(F32)
    return high, middle, rest - middle


def take_lanes(table, lanes):
    return jnp.take_along_axis(table, lanes, axis=1, mode="promise_in_bounds")


def inverse_sym(matrix):
    cofactor = [
        matrix[3] * matrix[5] - matrix[4] * matrix[4],
        matrix[2] * matrix[4] - matrix[1] * matrix[5],
        matrix[1] * matrix[4] - matrix[2] * matrix[3],
        matrix[0] * matrix[5] - matrix[2] * matrix[2],
        matrix[1] * matrix[2] - matrix[0] * matrix[4],
        matrix[0] * matrix[3] - matrix[1] * matrix[1],
    ]
    determinant = matrix[0] * cofactor[0] + matrix[1] * cofactor[1] + matrix[2] * cofactor[2]
    return [cofactor_entry / determinant for cofactor_entry in cofactor]


def apply_sym(inverse, comp_one, comp_two, comp_three):
    return [
        inverse[0] * comp_one + inverse[1] * comp_two + inverse[2] * comp_three,
        inverse[1] * comp_one + inverse[3] * comp_two + inverse[4] * comp_three,
        inverse[2] * comp_one + inverse[4] * comp_two + inverse[5] * comp_three,
    ]


def pack_kernel(
    num_hbm,
    den_hbm,
    bias_hbm,
    chain_hbm,
    list_hbm,
    counts_hbm,
    obs_hbm,
    prior_hbm,
    pick_hbm,
    point_hbm,
    out_ref,
    num_ref,
    den_ref,
    bias_ref,
    chain_ref,
    list_ref,
    counts_ref,
    obs_ref,
    prior_ref,
    pick_ref,
    point_ref,
    table_ref,
    listed_ref,
    sems,
):
    copies = [
        pltpu.make_async_copy(source, target, sems.at[index])
        for index, (source, target) in enumerate(
            [
                (num_hbm, num_ref),
                (den_hbm, den_ref),
                (bias_hbm, bias_ref),
                (chain_hbm, chain_ref),
                (list_hbm, list_ref),
                (counts_hbm, counts_ref),
                (obs_hbm, obs_ref),
                (prior_hbm, prior_ref),
                (pick_hbm, pick_ref),
                (point_hbm, point_ref),
            ]
        )
    ]
    for copy in copies:
        copy.start()
    owners = out_ref.shape[0] // BUCKET_ROWS
    scenes = num_ref.shape[1]
    listed = list_ref.shape[1]
    table_ref[...] = jnp.zeros(table_ref.shape, F32)
    for copy in copies[:5]:
        copy.wait()
    numer = num_ref[...].astype(F32)
    denom = den_ref[...].astype(F32)
    for which in range(2):
        table_ref[16 * which : 16 * which + 16, :] = numer[20 * which : 20 * which + 16]
        table_ref[33 + 16 * which : 48 + 16 * which, :] = denom[19 * which : 19 * which + 15]
        late = LATE_TERMS + 4 * which
        table_ref[late : late + 4, :] = numer[20 * which + 16 : 20 * which + 20]
        table_ref[late + 8 : late + 12, :] = denom[19 * which + 15 : 19 * which + 19]
    for part, value in enumerate(split3(bias_ref[...])):
        first = BIAS_ROW + part * SUB
        table_ref[first : first + 6, :] = value
    place = (chain_ref[...] & (scenes - 1)) + (lane_iota((1, scenes)) // (scenes // 4)) * scenes
    table_ref[CHAIN_ROW : CHAIN_ROW + 1, :] = (place >> 8).astype(F32)
    table_ref[CHAIN_ROW + 1 : CHAIN_ROW + 2, :] = (place & 255).astype(F32)
    table = table_ref[...].astype(BF16)
    for first in range(0, listed, 256):
        chosen = jnp.broadcast_to(list_ref[:, first : first + 256], (scenes, 256))
        onehot = jnp.where(chosen == sublane_iota((scenes, 256)), 1.0, 0.0).astype(BF16)
        got = jnp.dot(table, onehot, preferred_element_type=F32)
        bias_rows = sum(
            got[BIAS_ROW + part * SUB : BIAS_ROW + (part + 1) * SUB] for part in range(1, 3)
        ) + got[BIAS_ROW : BIAS_ROW + SUB]
        got = jnp.concatenate([got[:BIAS_ROW], bias_rows, got[CHAIN_ROW:]], axis=0)
        got = jnp.concatenate([got, jnp.zeros((LANES - got.shape[0], 256), F32)], axis=0)
        for part in range(0, 256, LANES):
            listed_ref[first + part : first + part + LANES, :] = got[:, part : part + LANES].T
    for copy in copies[5:]:
        copy.wait()
    counts = jnp.broadcast_to(counts_ref[...].astype(F32), (owners, owners)).T
    slot = lane_iota((SUB, LANES)).astype(F32)
    lane = lane_iota((SUB, LANES))
    for group in range(owners // SUB):
        live_count = counts[group * SUB : (group + 1) * SUB, :1]
        base = group * SUB * BUCKET_ROWS

        def put(row, value):
            out_ref[pl.ds(base + row, SUB, stride=BUCKET_ROWS), :] = value

        for row in range(4):
            put(row, obs_ref[pl.ds(group * SUB * 4 + row, SUB, stride=4), :])
        for half in range(2):
            rows = pl.ds(group * SUB * 2 + half, SUB, stride=2)
            live = slot + float(half * LANES) < live_count
            put(4 + half, jnp.where(live, prior_ref[rows, :], 0.0))
            put(6 + half, (pick_ref[rows, :] * 2048 + point_ref[rows, :]).astype(F32))
        blocks = [listed_ref[pl.ds(group * SUB * 8 + k, SUB, stride=8), :] for k in range(8)]
        for bit in range(3):
            step = 1 << bit
            shift = step * SCENE_LANES
            odd = ((lane // SCENE_LANES) & step) != 0
            turned = list(blocks)
            for k in range(8):
                if k & step:
                    continue
                low, high = blocks[k], blocks[k + step]
                turned[k] = jnp.where(odd, pltpu.roll(high, shift, 1), low)
                turned[k + step] = jnp.where(odd, high, pltpu.roll(low, LANES - shift, 1))
            blocks = turned
        for block in range(SCENE_ROWS):
            put(8 + block, blocks[block])


def ratios(coef, east, north, up):
    east_sq, north_sq, up_sq = east * east, north * north, up * up
    east_north, east_up, north_up = east * north, east * up, north * up
    terms = [
        (1, None, None, None),
        (east, 1, None, None),
        (north, None, 1, None),
        (up, None, None, 1),
        (east_north, north, east, None),
        (east_up, up, None, east),
        (north_up, None, up, north),
        (east_sq, 2.0 * east, None, None),
        (north_sq, None, 2.0 * north, None),
        (up_sq, None, None, 2.0 * up),
        (east_north * up, north_up, east_up, east_north),
        (east_sq * east, 3.0 * east_sq, None, None),
        (east * north_sq, north_sq, 2.0 * east_north, None),
        (east * up_sq, up_sq, None, 2.0 * east_up),
        (east_sq * north, 2.0 * east_north, east_sq, None),
        (north_sq * north, None, 3.0 * north_sq, None),
        (north * up_sq, None, up_sq, 2.0 * north_up),
        (east_sq * up, 2.0 * east_up, None, east_sq),
        (north_sq * up, None, 2.0 * north_up, north_sq),
        (up_sq * up, None, None, 3.0 * up_sq),
    ]
    sums = [[None] * 4 for _ in range(4)]
    for cubic in (2, 3):
        sums[cubic][0] = jnp.ones_like(east)

    def add(cubic, term, row):
        if cubic >= 2 and term == 0:
            return
        value = coef(row)
        for which, factor in enumerate(terms[term]):
            if factor is None:
                continue
            product = value if isinstance(factor, int) else value * factor
            held = sums[cubic][which]
            sums[cubic][which] = product if held is None else held + product

    bias = []
    for word in range(SCENE_LANES):
        for cubic in range(4):
            add(cubic, word, cubic * SCENE_LANES + word)
        add(word // 4, 16 + word % 4, LATE_TERMS + word)
        if word < 6:
            bias.append(coef(BIAS_ROW + word))
    found = []
    for top, bottom in ((sums[0], sums[2]), (sums[1], sums[3])):
        quotient = top[0] / bottom[0]
        found.append(quotient)
        found.append(
            [(top[which] - quotient * bottom[which]) / bottom[0] for which in range(1, 4)]
        )
    return found, bias


def tile_kernel(
    got_ref,
    ground_ref,
    next_ref,
    out_ref,
    packed_ref,
    parts_even,
    parts_odd,
    sums_ref,
    table_ref,
    step_ref,
    total_ref,
    place_ref,
    halo_ref,
    coef_ref,
    *,
    strips,
):
    owners = got_ref.shape[0] // BUCKET_ROWS
    groups = owners // SUB
    tiles = owners // strips
    points = ground_ref.shape[1]
    point_rows = points // LANES
    vreg = (SUB, LANES)
    lane = lane_iota(vreg)

    def fill_table(value):
        for axis in range(3):
            for row in range(point_rows):
                at = (axis * point_rows + row) * SUB
                table_ref[at : at + SUB, :] = jnp.broadcast_to(value(axis, row), vreg)

    fill_table(lambda axis, row: ground_ref[axis : axis + 1, row * LANES : (row + 1) * LANES])

    def tie_row(group, row):
        return got_ref[pl.ds(group * (SUB * BUCKET_ROWS) + row, SUB, stride=BUCKET_ROWS), :]

    def code_of(group, half):
        code = tie_row(group, 6 + half).astype(I32)
        return code >> 11, code & (points - 1)

    def gather_points(point):
        high = point >> 7
        low = point & (LANES - 1)
        found = [None] * 3
        for row in range(point_rows):
            here = high == row
            for axis in range(3):
                at = (axis * point_rows + row) * SUB
                value = take_lanes(table_ref[at : at + SUB, :], low)
                found[axis] = value if row == 0 else jnp.where(here, value, found[axis])
        return found

    def turn_scenes(group):
        for block in range(SCENE_ROWS):
            value = tie_row(group, 8 + block)
            for word in range(SCENE_LANES if block < 5 else 6):
                at = (block * SCENE_LANES + word) * SUB
                coef_ref[at : at + SUB, :] = (
                    pltpu.roll(value, LANES - word, 1) if word else value
                )

    def first_pass(group, half, parts_ref):
        pick, point = code_of(group, half)
        first_lane = pick * SCENE_LANES
        east, north, up = gather_points(point)

        def coef(row):
            return take_lanes(coef_ref[row * SUB : (row + 1) * SUB, :], first_lane)

        line_obs = tie_row(group, 2 * half)
        samp_obs = tie_row(group, 2 * half + 1)
        prior = tie_row(group, 4 + half)
        (line_ratio, line_jac, samp_ratio, samp_jac), bias = ratios(coef, east, north, up)
        line_res = line_obs - (line_ratio + bias[0] + bias[1] * samp_obs + bias[2] * line_obs)
        samp_res = samp_obs - (samp_ratio + bias[3] + bias[4] * samp_obs + bias[5] * line_obs)
        weight = prior / (1.0 + (line_res * line_res + samp_res * samp_res) / cauchy_scale)
        place = pl.ds((group * 2 + half) * SUB, SUB)
        for row, value in enumerate([line_res, samp_res] + line_jac + samp_jac + [weight]):
            packed_ref[row, place, :] = value
        pairs = [(0, 0), (0, 1), (0, 2), (1, 1), (1, 2), (2, 2)]
        sums = [weight * (line_jac[a] * line_jac[b] + samp_jac[a] * samp_jac[b]) for a, b in pairs]
        sums += [weight * (line_jac[a] * line_res + samp_jac[a] * samp_res) for a in range(3)]

        def put(row, value):
            parts_ref[pl.ds(half * PART_ROWS + row, SUB, stride=2 * PART_ROWS), :] = value

        for row, value in enumerate(sums):
            for part, piece in enumerate(split3(value)):
                put(row * 3 + part, piece)
        put(27, (point >> 8).astype(F32))
        put(28, (point & 255).astype(F32))

    wide = (16, LANES)
    steps_iota = [
        (sublane_iota(wide) + 16 * row).astype(F32).astype(BF16) for row in range(16)
    ]
    one = jnp.ones(wide, BF16)
    zero = jnp.zeros(wide, BF16)

    def sum_pass(first_bucket, count, parts_ref):
        left = []
        right = []
        for bucket in range(first_bucket, first_bucket + count):
            for half in range(2):
                first = (bucket * 2 + half) * PART_ROWS
                values = parts_ref[first : first + PART_ROWS, :].astype(BF16)
                high = jnp.broadcast_to(parts_ref[first + 27 : first + 28, :], wide).astype(BF16)
                low = jnp.broadcast_to(parts_ref[first + 28 : first + 29, :], wide).astype(BF16)
                rows = []
                for index in range(8):
                    here = high == jnp.full(wide, index, BF16)
                    rows.append(jnp.where(here, values[:16], zero))
                    rows.append(jnp.where(here, values[16:], zero))
                left.append(jnp.concatenate(rows, axis=0))
                right.append(
                    jnp.concatenate(
                        [jnp.where(low == step, one, zero) for step in steps_iota], axis=0
                    )
                )
        product = lax.dot_general(
            jnp.concatenate(left, axis=1),
            jnp.concatenate(right, axis=1),
            (((1,), (1,)), ((), ())),
            preferred_element_type=F32,
        )
        for half in range(2):
            sums_ref[half] += product[:, half * LANES : (half + 1) * LANES]

    def both(group, lagging, parts_ref, lagging_ref):
        if group is not None:
            turn_scenes(group)
        for half in range(2):
            if lagging:
                sum_pass(half * 4, 4, lagging_ref)
            if group is not None:
                first_pass(group, half, parts_ref)

    for ref in (parts_even, parts_odd):
        ref[...] = jnp.zeros(ref.shape, F32)
    sums_ref[...] = jnp.zeros(sums_ref.shape, F32)
    both(0, False, parts_even, None)

    def pair_of_groups(pair, carry):
        both(2 * pair + 1, True, parts_odd, parts_even)
        both(2 * pair + 2, True, parts_even, parts_odd)
        return carry

    lax.fori_loop(0, groups // 2 - 1, pair_of_groups, 0)
    both(groups - 1, True, parts_odd, parts_even)
    both(None, True, None, parts_odd)

    def point_sum(row, half):
        return sum(
            sums_ref[half, pl.ds(row * 3 + part, SUB, stride=PART_ROWS), :] for part in (2, 1, 0)
        )

    for half in range(2):
        sums = [point_sum(row, half) for row in range(9)]
        matrix = [
            sums[0] + point_damping,
            sums[1],
            sums[2],
            sums[3] + point_damping,
            sums[4],
            sums[5] + point_damping,
        ]
        steps = apply_sym(inverse_sym(matrix), sums[6], sums[7], sums[8])
        for axis in range(3):
            step_ref[pl.ds(axis * point_rows + half, SUB, stride=2), :] = steps[axis]
    for axis in range(3):
        for row in range(point_rows):
            columns = slice(row * LANES, (row + 1) * LANES)
            at = axis * point_rows + row
            next_ref[axis : axis + 1, columns] = (
                ground_ref[axis : axis + 1, columns] + step_ref[at : at + 1, :]
            )
    fill_table(
        lambda axis, row: step_ref[axis * point_rows + row : axis * point_rows + row + 1, :]
    )

    def second_pass(group, carry):
        rows = []
        picks = []
        for half in range(2):
            pick, point = code_of(group, half)
            tie_step = gather_points(point)
            place = pl.ds((group * 2 + half) * SUB, SUB)
            packed = [packed_ref[row, place, :] for row in range(9)]
            line_obs = tie_row(group, 2 * half)
            samp_obs = tie_row(group, 2 * half + 1)
            weight = packed[8]
            line_res = packed[0] - (
                packed[2] * tie_step[0] + packed[3] * tie_step[1] + packed[4] * tie_step[2]
            )
            samp_res = packed[1] - (
                packed[5] * tie_step[0] + packed[6] * tie_step[1] + packed[7] * tie_step[2]
            )
            samp_weight = weight * samp_obs
            line_weight = weight * line_obs
            rows.append(
                [
                    weight,
                    samp_weight,
                    line_weight,
                    samp_weight * samp_obs,
                    samp_weight * line_obs,
                    line_weight * line_obs,
                    weight * line_res,
                    samp_weight * line_res,
                    line_weight * line_res,
                    weight * samp_res,
                    samp_weight * samp_res,
                    line_weight * samp_res,
                ]
            )
            picks.append(pick)
        total = jnp.zeros(vreg, F32)
        for scene in range(8):
            first, second = picks[0] == scene, picks[1] == scene
            for row in range(12):
                value = jnp.where(first, rows[0][row], 0.0) + jnp.where(second, rows[1][row], 0.0)
                total = jnp.where(
                    lane == scene * SCENE_LANES + row,
                    jnp.sum(value, axis=1, keepdims=True),
                    total,
                )
        place = pl.ds(group * SUB, SUB)
        total_ref[place, :] = total
        chain = tie_row(group, 8 + CHAIN_SENT // SCENE_LANES)
        chain_lane = (lane // SCENE_LANES) * SCENE_LANES + CHAIN_SENT % SCENE_LANES
        place_ref[place, :] = take_lanes(chain, chain_lane) * 256.0 + take_lanes(
            chain, chain_lane + 1
        )
        return carry

    lax.fori_loop(0, groups, second_pass, 0, unroll=2)

    segment = 4 * LANES
    word = lane % SCENE_LANES
    stacked = []
    for near in range(HALO):
        rows = []
        for strip in range(strips):
            for side in range(2):
                at = float(strip * segment + (near if side else segment - HALO + near))
                for block in range(0, tiles, SUB):
                    here = [pl.ds(s * tiles + block, SUB) for s in range(strips)]
                    rows.append(
                        sum(jnp.where(place_ref[h, :] == at, total_ref[h, :], 0.0) for h in here)
                    )
        stacked.append(jnp.concatenate(rows, axis=0))
    stacked = jnp.concatenate(stacked, axis=1)
    source = sublane_iota((HALO * LANES, 2 * LANES))
    target = lane_iota((HALO * LANES, 2 * LANES))
    chosen = (source % SCENE_LANES == target // SCENE_LANES) & (
        target % SCENE_LANES == source // LANES + POS_LANE + 1
    )
    chosen = jnp.where(chosen, 1.0, 0.0).astype(BF16)
    moved = sum(
        jnp.dot(part.astype(BF16), chosen, preferred_element_type=F32)
        for part in reversed(split3(stacked))
    )
    flag = lane // SCENE_LANES == 4
    for side in range(2):
        for part in range(2):
            for strip in range(strips):
                slot = strip * 4 + side * 2 + part
                edge = tiles if side else SUB
                halo_ref[slot, edge : edge + SUB, :] = jnp.zeros(vreg, F32)
                for block in range(0, tiles, SUB):
                    at = (strip * 2 + side) * tiles + block
                    value = moved[at : at + SUB, part * LANES : (part + 1) * LANES]
                    if part:
                        value = jnp.where(flag, 1.0, value)
                    first = SUB + block + (-1 if side else 1)
                    halo_ref[slot, first : first + SUB, :] = value
    for strip in range(strips):
        start = float(strip * segment)
        for block in range(0, tiles, SUB):
            for source in range(strips):
                place = place_ref[pl.ds(source * tiles + block, SUB), :] - start
                inside = (place >= 0.0) & (place < float(segment))
                value = total_ref[pl.ds(source * tiles + block, SUB), :]
                value = jnp.where(word == POS_LANE, jnp.where(inside, place, -1.0), value)
                value = jnp.where(
                    word > POS_LANE,
                    halo_ref[strip * 4 + source, SUB + block : 2 * SUB + block, :],
                    value,
                )
                out_ref[
                    pl.ds((strip * tiles + block) * strips + source, SUB, stride=strips), :
                ] = value


def chain_kernel(got_ref, out_ref, turned_ref, *, coupling):
    scenes = out_ref.shape[1]
    total = jnp.zeros((3 * SCENE_LANES, scenes), F32)
    border = jnp.zeros((SUB, LANES), F32)
    for first in range(0, got_ref.shape[0], LANES):
        block = got_ref[first : first + LANES, :]
        for row in range(0, LANES, SUB):
            border = border + block[row : row + SUB]
        turned = block.T
        values = jnp.concatenate(
            [turned[k * SCENE_LANES : (k + 1) * SCENE_LANES] for k in range(8)], axis=1
        )
        position = values[POS_LANE : POS_LANE + 1].astype(I32)
        onehot = jnp.where(
            jnp.broadcast_to(position, (scenes, 8 * LANES)) == sublane_iota((scenes, 8 * LANES)),
            1.0,
            0.0,
        ).astype(BF16)
        pieces = jnp.concatenate(split3(values), axis=0).astype(BF16)
        total = total + lax.dot_general(
            pieces, onehot, (((1,), (1,)), ((), ())), preferred_element_type=F32
        )
    sums = total[32:48] + total[16:32] + total[:16]
    sums = jnp.where(sublane_iota(sums.shape) == POS_LANE, 1.0, sums)

    border = border + pltpu.roll(border, 4, 0)
    turned_ref[...] = jnp.concatenate([border] * (LANES // SUB), axis=0).T
    lane = lane_iota((SUB, LANES))
    sides = []
    for side in range(2):
        parts = []
        for part in range(2):
            value = jnp.zeros((SUB, LANES), F32)
            for near in range(HALO):
                column = turned_ref[pl.ds(POS_LANE + 1 + near, SUB, stride=SCENE_LANES), :]
                row = side * 2 + part
                here = lane == (near if side else LANES - HALO + near)
                value = jnp.where(here, column[:, row : row + 1], value)
            parts.append(value)
        sides.append(jnp.concatenate(parts, axis=0))
    sums = jnp.concatenate([sides[0], sums, sides[1]], axis=1)
    width = sums.shape[1]
    rows = [sums[row : row + 1] for row in range(13)]
    matrix = [
        rows[0] + 2.0 * coupling,
        rows[1],
        rows[2],
        rows[3] + 2.0 * coupling,
        rows[4],
        rows[5] + 2.0 * coupling,
    ]
    exists = rows[POS_LANE] > 0.0
    inverse = [jnp.where(exists, entry, 0.0) for entry in inverse_sym(matrix)]

    def apply_pair(vectors):
        return apply_sym(inverse, *vectors[:3]) + apply_sym(inverse, *vectors[3:])

    right_sides = rows[6:12]
    smoothed = apply_pair(right_sides)
    for _ in range(SWEEPS - 1):
        smoothed = apply_pair(
            [
                side + coupling * (pltpu.roll(value, 1, 1) + pltpu.roll(value, width - 1, 1))
                for side, value in zip(right_sides, smoothed)
            ]
        )
    for row in range(6):
        out_ref[row : row + 1, :] = smoothed[row][:, LANES : LANES + scenes]


def call(kernel, out_shape, scratch=(), name=None, vmem=48, **specs):
    return pl.pallas_call(
        kernel,
        out_shape=out_shape,
        scratch_shapes=list(scratch),
        compiler_params=pltpu.CompilerParams(vmem_limit_bytes=vmem * 1024 * 1024),
        name=name,
        **specs,
    )


def shape(dims, dtype=F32):
    return jax.ShapeDtypeStruct(dims, dtype)


def tile_call(got, ground, strips):
    owners = got.shape[0] // BUCKET_ROWS
    tie_rows = owners * 2
    points = ground.shape[1]
    return call(
        functools.partial(tile_kernel, strips=strips),
        (shape(ground.shape), shape((owners * strips, LANES))),
        [
            pltpu.VMEM((9, tie_rows, LANES), F32),
            pltpu.VMEM((2 * SUB * PART_ROWS, LANES), F32),
            pltpu.VMEM((2 * SUB * PART_ROWS, LANES), F32),
            pltpu.VMEM((2, SUB * PART_ROWS, LANES), F32),
            pltpu.VMEM((3 * points // LANES * SUB, LANES), F32),
            pltpu.VMEM((3 * points // LANES, LANES), F32),
            pltpu.VMEM((owners, LANES), F32),
            pltpu.VMEM((owners, LANES), F32),
            pltpu.VMEM((strips * 4, owners // strips + 2 * SUB, LANES), F32),
            pltpu.VMEM((SCENE_ROWS * SCENE_LANES * SUB, LANES), F32),
        ],
        name="tile_sums",
    )(got, ground)


def per_device(
    num_coef,
    den_coef,
    bias,
    scene_chain,
    bucket_scenes,
    tie_counts,
    tie_obs,
    tie_prior,
    tie_pick,
    tie_point,
    ground,
):
    strips = lax.axis_size("strip")
    tiles = lax.axis_size("tile")
    owners = strips * tiles
    tie_dev = tie_prior.shape[0]
    tie_rows = tie_dev // LANES
    scenes_dev = num_coef.shape[1]
    listed = bucket_scenes.shape[1]
    coupling = smooth_gain * (tie_dev // scenes_dev)

    arguments = [
        num_coef,
        den_coef,
        bias,
        scene_chain.reshape(1, scenes_dev),
        bucket_scenes,
        tie_counts,
        tie_obs.reshape(2, tie_rows, LANES).transpose(1, 0, 2).reshape(2 * tie_rows, LANES),
        tie_prior.reshape(tie_rows, LANES),
        tie_pick.reshape(tie_rows, LANES),
        tie_point.reshape(tie_rows, LANES),
    ]
    sent = call(
        pack_kernel,
        shape((owners * BUCKET_ROWS, LANES)),
        [pltpu.VMEM(argument.shape, argument.dtype) for argument in arguments]
        + [
            pltpu.VMEM((LANES, scenes_dev), F32),
            pltpu.VMEM((listed, LANES), F32),
            pltpu.SemaphoreType.DMA((len(arguments),)),
        ],
        name="pack",
        vmem=64,
        in_specs=[pl.BlockSpec(memory_space=pltpu.HBM)] * len(arguments),
    )(*arguments)
    got = lax.all_to_all(
        sent.reshape(owners, BUCKET_ROWS // 2, 2, LANES), AXES, 0, 0, tiled=True
    ).reshape(owners * BUCKET_ROWS, LANES)
    ground_next, totals = tile_call(got, ground, strips)
    got_totals = lax.all_to_all(totals.reshape(owners, strips, LANES), AXES, 0, 0, tiled=True)
    smoothed = call(
        functools.partial(chain_kernel, coupling=coupling),
        shape((6, scenes_dev)),
        [pltpu.VMEM((LANES, LANES), F32)],
        name="chain",
    )(got_totals.reshape(owners * strips, LANES))
    return ground_next, smoothed


def solution(mesh):
    in_specs = (
        P(None, AXES),
        P(None, AXES),
        P(None, AXES),
        P(AXES),
        P(AXES, None),
        P(AXES, None),
        P(None, AXES),
        P(AXES),
        P(AXES),
        P(AXES),
        P(None, AXES),
    )
    out_specs = (P(None, AXES), P(None, AXES))
    return jax.shard_map(
        per_device, mesh=mesh, in_specs=in_specs, out_specs=out_specs, check_vma=False
    )
```

```python
import functools

import jax
import jax.numpy as jnp
from jax import lax
from jax.experimental import pallas as pl
from jax.experimental.pallas import tpu as pltpu
from jax.sharding import PartitionSpec as P

SWEEPS = 4
AXES = ("strip", "tile")
F32 = jnp.float32
BF16 = jnp.bfloat16
I32 = jnp.int32
LANES = 128
SUB = 8

cauchy_scale = 1.0
point_damping = 1.0
smooth_gain = 0.25

LATE_TERMS = 64
BIAS_ROW = 80
CHAIN_ROW = 104
CHAIN_SENT = 88
SCENE_ROWS = 6
LANE_STEP = 2
BUCKET_ROWS = 8 + SCENE_ROWS
SCENE_LANES = 16
POS_LANE = 12
TOGETHER = 16
HALO = SWEEPS - 1
PART_ROWS = 32
TERM_ROWS = 20
BUCKET_PARTS = 68


def lane_iota(shape):
    return lax.broadcasted_iota(I32, shape, len(shape) - 1)


def sublane_iota(shape):
    return lax.broadcasted_iota(I32, shape, len(shape) - 2)


def split3(value):
    high = value.astype(BF16).astype(F32)
    rest = value - high
    middle = rest.astype(BF16).astype(F32)
    return high, middle, rest - middle


def one_hot_rows(low):
    wide = (16, low.shape[1])
    held = jnp.broadcast_to(low, wide).astype(BF16)
    one = jnp.ones(wide, BF16)
    zero = jnp.zeros(wide, BF16)
    rows = sublane_iota(wide)
    return jnp.concatenate(
        [
            jnp.where(held == (rows + first).astype(F32).astype(BF16), one, zero)
            for first in range(0, 256, 16)
        ],
        axis=0,
    )


def take_lanes(table, lanes):
    return jnp.take_along_axis(table, lanes, axis=1, mode="promise_in_bounds")


def inverse_sym(matrix):
    cofactor = [
        matrix[3] * matrix[5] - matrix[4] * matrix[4],
        matrix[2] * matrix[4] - matrix[1] * matrix[5],
        matrix[1] * matrix[4] - matrix[2] * matrix[3],
        matrix[0] * matrix[5] - matrix[2] * matrix[2],
        matrix[1] * matrix[2] - matrix[0] * matrix[4],
        matrix[0] * matrix[3] - matrix[1] * matrix[1],
    ]
    determinant = matrix[0] * cofactor[0] + matrix[1] * cofactor[1] + matrix[2] * cofactor[2]
    return [cofactor_entry / determinant for cofactor_entry in cofactor]


def apply_sym(inverse, comp_one, comp_two, comp_three):
    return [
        inverse[0] * comp_one + inverse[1] * comp_two + inverse[2] * comp_three,
        inverse[1] * comp_one + inverse[3] * comp_two + inverse[4] * comp_three,
        inverse[2] * comp_one + inverse[4] * comp_two + inverse[5] * comp_three,
    ]


def pack_kernel(
    num_hbm,
    den_hbm,
    bias_hbm,
    chain_hbm,
    list_hbm,
    counts_hbm,
    obs_hbm,
    prior_hbm,
    pick_hbm,
    point_hbm,
    out_ref,
    num_ref,
    den_ref,
    bias_ref,
    chain_ref,
    list_ref,
    counts_ref,
    obs_ref,
    prior_ref,
    pick_ref,
    point_ref,
    table_ref,
    sems,
):
    copies = [
        pltpu.make_async_copy(source, target, sems.at[index])
        for index, (source, target) in enumerate(
            [
                (num_hbm, num_ref),
                (den_hbm, den_ref),
                (bias_hbm, bias_ref),
                (chain_hbm, chain_ref),
                (list_hbm, list_ref),
                (counts_hbm, counts_ref),
                (obs_hbm, obs_ref),
                (prior_hbm, prior_ref),
                (pick_hbm, pick_ref),
                (point_hbm, point_ref),
            ]
        )
    ]
    for copy in copies:
        copy.start()
    owners = out_ref.shape[0] // BUCKET_ROWS
    scenes = num_ref.shape[1]
    listed = list_ref.shape[1]
    table_ref[...] = jnp.zeros(table_ref.shape, F32)
    for copy in copies[:5]:
        copy.wait()
    numer = num_ref[...].astype(F32)
    denom = den_ref[...].astype(F32)
    for which in range(2):
        table_ref[16 * which : 16 * which + 16, :] = numer[20 * which : 20 * which + 16]
        table_ref[33 + 16 * which : 48 + 16 * which, :] = denom[19 * which : 19 * which + 15]
        late = LATE_TERMS + 4 * which
        table_ref[late : late + 4, :] = numer[20 * which + 16 : 20 * which + 20]
        table_ref[late + 8 : late + 12, :] = denom[19 * which + 15 : 19 * which + 19]
    for part, value in enumerate(split3(bias_ref[...])):
        first = BIAS_ROW + part * SUB
        table_ref[first : first + 6, :] = value
    place = (chain_ref[...] & (scenes - 1)) + (lane_iota((1, scenes)) // (scenes // 4)) * scenes
    table_ref[CHAIN_ROW : CHAIN_ROW + 1, :] = (place >> 8).astype(F32)
    table_ref[CHAIN_ROW + 1 : CHAIN_ROW + 2, :] = (place & 255).astype(F32)
    table = table_ref[...].astype(BF16)
    lane = lane_iota((SUB, LANES))
    per_row = LANES // SUB
    index = (lane % per_row) * SUB + sublane_iota((SUB, LANES))
    lists = jnp.zeros((SUB, LANES), F32)
    for row in range(listed // LANES):
        ids = list_ref[:, row * LANES : (row + 1) * LANES].astype(F32)
        found = take_lanes(jnp.broadcast_to(ids, (SUB, LANES)), index)
        lists = jnp.where(lane // per_row == row, found, lists)
    lows = []
    for first in range(0, scenes, 256):
        inside = (lists >= float(first)) & (lists < float(first + 256))
        lows.append(jnp.where(inside, lists - float(first), -1.0))
    got = []
    for pair in range(0, SUB, 2):
        onehot = []
        for k in (pair, pair + 1):
            onehot.append(
                jnp.concatenate([one_hot_rows(low[k : k + 1]) for low in lows], axis=0)
            )
        both = jnp.dot(
            table, jnp.concatenate(onehot, axis=1), preferred_element_type=F32
        )
        for part in range(0, 256, LANES):
            one = both[:, part : part + LANES]
            bias_rows = (
                one[BIAS_ROW : BIAS_ROW + SUB]
                + one[BIAS_ROW + SUB : BIAS_ROW + 2 * SUB]
                + one[BIAS_ROW + 2 * SUB : BIAS_ROW + 3 * SUB]
            )
            got.append(jnp.concatenate([one[:BIAS_ROW], bias_rows, one[CHAIN_ROW:]], axis=0))
    for block in range(SCENE_ROWS):
        words = slice(block * SCENE_LANES, (block + 1) * SCENE_LANES)
        turned = jnp.concatenate([one[words] for one in got], axis=0).T
        for group in range(owners // SUB):
            out_ref[
                pl.ds(group * SUB * BUCKET_ROWS + 8 + block, SUB, stride=BUCKET_ROWS), :
            ] = turned[group * SUB : (group + 1) * SUB]
    for copy in copies[5:]:
        copy.wait()
    counts = jnp.broadcast_to(counts_ref[...].astype(F32), (owners, owners)).T
    slot = lane.astype(F32)
    for group in range(owners // SUB):
        live_count = counts[group * SUB : (group + 1) * SUB, :1]
        base = group * SUB * BUCKET_ROWS

        def put(row, value):
            out_ref[pl.ds(base + row, SUB, stride=BUCKET_ROWS), :] = value

        for row in range(4):
            put(row, obs_ref[pl.ds(group * SUB * 4 + row, SUB, stride=4), :])
        for half in range(2):
            rows = pl.ds(group * SUB * 2 + half, SUB, stride=2)
            live = slot + float(half * LANES) < live_count
            put(4 + half, jnp.where(live, prior_ref[rows, :], 0.0))
            put(6 + half, (pick_ref[rows, :] * 2048 + point_ref[rows, :]).astype(F32))


def ratios(coef, east, north, up):
    east_sq, north_sq, up_sq = east * east, north * north, up * up
    east_north, east_up, north_up = east * north, east * up, north * up
    terms = [
        (1, None, None, None),
        (east, 1, None, None),
        (north, None, 1, None),
        (up, None, None, 1),
        (east_north, north, east, None),
        (east_up, up, None, east),
        (north_up, None, up, north),
        (east_sq, 2.0 * east, None, None),
        (north_sq, None, 2.0 * north, None),
        (up_sq, None, None, 2.0 * up),
        (east_north * up, north_up, east_up, east_north),
        (east_sq * east, 3.0 * east_sq, None, None),
        (east * north_sq, north_sq, 2.0 * east_north, None),
        (east * up_sq, up_sq, None, 2.0 * east_up),
        (east_sq * north, 2.0 * east_north, east_sq, None),
        (north_sq * north, None, 3.0 * north_sq, None),
        (north * up_sq, None, up_sq, 2.0 * north_up),
        (east_sq * up, 2.0 * east_up, None, east_sq),
        (north_sq * up, None, 2.0 * north_up, north_sq),
        (up_sq * up, None, None, 3.0 * up_sq),
    ]
    sums = [[None] * 4 for _ in range(4)]
    for cubic in (2, 3):
        sums[cubic][0] = jnp.ones_like(east)

    def add(cubic, term, row):
        if cubic >= 2 and term == 0:
            return
        value = coef(row)
        for which, factor in enumerate(terms[term]):
            if factor is None:
                continue
            product = value if isinstance(factor, int) else value * factor
            held = sums[cubic][which]
            sums[cubic][which] = product if held is None else held + product

    words = [w for first in range(LANE_STEP) for w in range(first, SCENE_LANES, LANE_STEP)]
    bias = [None] * 6
    for word in words:
        for cubic in range(4):
            add(cubic, word, cubic * SCENE_LANES + word)
        add(word // 4, 16 + word % 4, LATE_TERMS + word)
        if word < 6:
            bias[word] = coef(BIAS_ROW + word)
    found = []
    for top, bottom in ((sums[0], sums[2]), (sums[1], sums[3])):
        quotient = top[0] / bottom[0]
        found.append(quotient)
        found.append(
            [(top[which] - quotient * bottom[which]) / bottom[0] for which in range(1, 4)]
        )
    return found, bias


def tile_kernel(
    got_ref,
    ground_ref,
    next_ref,
    out_ref,
    packed_ref,
    parts_even,
    parts_odd,
    sums_ref,
    table_ref,
    step_ref,
    total_ref,
    place_ref,
    halo_ref,
    coef_ref,
    terms_ref,
    scene_ref,
    *,
    strips,
):
    owners = got_ref.shape[0] // BUCKET_ROWS
    groups = owners // SUB
    tiles = owners // strips
    points = ground_ref.shape[1]
    point_rows = points // LANES
    vreg = (SUB, LANES)
    lane = lane_iota(vreg)

    def fill_table(value):
        for axis in range(3):
            for row in range(point_rows):
                at = (axis * point_rows + row) * SUB
                table_ref[at : at + SUB, :] = jnp.broadcast_to(value(axis, row), vreg)

    fill_table(lambda axis, row: ground_ref[axis : axis + 1, row * LANES : (row + 1) * LANES])

    def tie_row(group, row):
        return got_ref[pl.ds(group * (SUB * BUCKET_ROWS) + row, SUB, stride=BUCKET_ROWS), :]

    def code_of(group, half):
        code = tie_row(group, 6 + half).astype(I32)
        return code >> 11, code & (points - 1)

    def gather_points(point):
        high = point >> 7
        low = point & (LANES - 1)
        found = [None] * 3
        for row in range(point_rows):
            here = high == row
            for axis in range(3):
                at = (axis * point_rows + row) * SUB
                value = take_lanes(table_ref[at : at + SUB, :], low)
                found[axis] = value if row == 0 else jnp.where(here, value, found[axis])
        return found

    def turn_scenes(group):
        for block in range(SCENE_ROWS):
            value = tie_row(group, 8 + block)
            for word in range(0, SCENE_LANES if block < 5 else 6, LANE_STEP):
                at = (block * SCENE_LANES + word) * SUB
                coef_ref[at : at + SUB, :] = (
                    pltpu.roll(value, LANES - word, 1) if word else value
                )

    def first_pass(group, half, parts_ref):
        pick, point = code_of(group, half)
        first_lane = pick * SCENE_LANES
        east, north, up = gather_points(point)

        def coef(row):
            at = (row - row % LANE_STEP) * SUB
            return take_lanes(coef_ref[at : at + SUB, :], first_lane + row % LANE_STEP)

        line_obs = tie_row(group, 2 * half)
        samp_obs = tie_row(group, 2 * half + 1)
        prior = tie_row(group, 4 + half)
        (line_ratio, line_jac, samp_ratio, samp_jac), bias = ratios(coef, east, north, up)
        line_res = line_obs - (line_ratio + bias[0] + bias[1] * samp_obs + bias[2] * line_obs)
        samp_res = samp_obs - (samp_ratio + bias[3] + bias[4] * samp_obs + bias[5] * line_obs)
        weight = prior / (1.0 + (line_res * line_res + samp_res * samp_res) / cauchy_scale)
        place = pl.ds((group * 2 + half) * SUB, SUB)
        for row, value in enumerate([line_res, samp_res] + line_jac + samp_jac + [weight]):
            packed_ref[row, place, :] = value
        pairs = [(0, 0), (0, 1), (0, 2), (1, 1), (1, 2), (2, 2)]
        sums = [weight * (line_jac[a] * line_jac[b] + samp_jac[a] * samp_jac[b]) for a, b in pairs]
        sums += [weight * (line_jac[a] * line_res + samp_jac[a] * samp_res) for a in range(3)]

        def put(row, value):
            parts_ref[pl.ds(half * PART_ROWS + row, SUB, stride=BUCKET_PARTS), :] = value

        for row, value in enumerate(sums):
            for part, piece in enumerate(split3(value)):
                put(row * 3 + part, piece)
        put(27, (point >> 8).astype(F32))
        put(28, (point & 255).astype(F32))

    wide = (16, LANES)
    steps_iota = [
        (sublane_iota(wide) + 16 * row).astype(F32).astype(BF16) for row in range(16)
    ]
    one = jnp.ones(wide, BF16)
    zero = jnp.zeros(wide, BF16)

    def product_of(first_bucket, count, parts_ref):
        left = []
        right = []
        for bucket in range(first_bucket, first_bucket + count):
            for half in range(2):
                first = bucket * BUCKET_PARTS + half * PART_ROWS
                values = parts_ref[first : first + PART_ROWS, :].astype(BF16)
                high = jnp.broadcast_to(parts_ref[first + 27 : first + 28, :], wide).astype(BF16)
                low = jnp.broadcast_to(parts_ref[first + 28 : first + 29, :], wide).astype(BF16)
                rows = []
                for index in range(8):
                    here = high == jnp.full(wide, index, BF16)
                    rows.append(jnp.where(here, values[:16], zero))
                    rows.append(jnp.where(here, values[16:], zero))
                left.append(jnp.concatenate(rows, axis=0))
                right.append(
                    jnp.concatenate(
                        [jnp.where(low == step, one, zero) for step in steps_iota], axis=0
                    )
                )
        return lax.dot_general(
            jnp.concatenate(left, axis=1),
            jnp.concatenate(right, axis=1),
            (((1,), (1,)), ((), ())),
            preferred_element_type=F32,
        )

    def sum_pass(first_bucket, count, parts_ref):
        products = [
            product_of(first_bucket + part * count // 2, count // 2, parts_ref)
            for part in range(2)
        ]
        product = products[0] + products[1]
        for half in range(2):
            sums_ref[half] += product[:, half * LANES : (half + 1) * LANES]

    def both(group, lagging, parts_ref, lagging_ref):
        if group is not None:
            turn_scenes(group)
        if lagging:
            sum_pass(0, SUB, lagging_ref)
        for half in range(2):
            if group is not None:
                first_pass(group, half, parts_ref)

    for ref in (parts_even, parts_odd):
        ref[...] = jnp.zeros(ref.shape, F32)
    sums_ref[...] = jnp.zeros(sums_ref.shape, F32)
    both(0, False, parts_even, None)

    def pair_of_groups(pair, carry):
        both(2 * pair + 1, True, parts_odd, parts_even)
        both(2 * pair + 2, True, parts_even, parts_odd)
        return carry

    lax.fori_loop(0, groups // 2 - 1, pair_of_groups, 0)
    both(groups - 1, True, parts_odd, parts_even)
    both(None, True, None, parts_odd)

    def point_sum(row, half):
        return sum(
            sums_ref[half, pl.ds(row * 3 + part, SUB, stride=PART_ROWS), :] for part in (2, 1, 0)
        )

    for half in range(2):
        sums = [point_sum(row, half) for row in range(9)]
        matrix = [
            sums[0] + point_damping,
            sums[1],
            sums[2],
            sums[3] + point_damping,
            sums[4],
            sums[5] + point_damping,
        ]
        steps = apply_sym(inverse_sym(matrix), sums[6], sums[7], sums[8])
        for axis in range(3):
            step_ref[pl.ds(axis * point_rows + half, SUB, stride=2), :] = steps[axis]
    for axis in range(3):
        for row in range(point_rows):
            columns = slice(row * LANES, (row + 1) * LANES)
            at = axis * point_rows + row
            next_ref[axis : axis + 1, columns] = (
                ground_ref[axis : axis + 1, columns] + step_ref[at : at + 1, :]
            )
    fill_table(
        lambda axis, row: step_ref[axis * point_rows + row : axis * point_rows + row + 1, :]
    )

    terms_ref[...] = jnp.zeros(terms_ref.shape, F32)
    scene_ref[...] = jnp.zeros(scene_ref.shape, F32)

    def tie_terms(group, slot):
        rows = []
        picks = []
        for half in range(2):
            pick, point = code_of(group, half)
            tie_step = gather_points(point)
            place = pl.ds((group * 2 + half) * SUB, SUB)
            packed = [packed_ref[row, place, :] for row in range(9)]
            line_obs = tie_row(group, 2 * half)
            samp_obs = tie_row(group, 2 * half + 1)
            weight = packed[8]
            line_res = packed[0] - (
                packed[2] * tie_step[0] + packed[3] * tie_step[1] + packed[4] * tie_step[2]
            )
            samp_res = packed[1] - (
                packed[5] * tie_step[0] + packed[6] * tie_step[1] + packed[7] * tie_step[2]
            )
            samp_weight = weight * samp_obs
            line_weight = weight * line_obs
            rows.append(
                [
                    weight,
                    samp_weight,
                    line_weight,
                    samp_weight * samp_obs,
                    samp_weight * line_obs,
                    line_weight * line_obs,
                    weight * line_res,
                    samp_weight * line_res,
                    line_weight * line_res,
                    weight * samp_res,
                    samp_weight * samp_res,
                    line_weight * samp_res,
                ]
            )
            picks.append(pick)
        for half in range(2):
            for row, value in enumerate(rows[half] + [picks[half].astype(F32)]):
                terms_ref[slot * 2 + half, pl.ds(row, SUB, stride=TERM_ROWS), :] = value

    def scene_sums(group, slot):
        for bucket in range(SUB):
            chosen = []
            pieces = [[], [], []]
            for half in range(2):
                first = bucket * TERM_ROWS
                pick = jnp.broadcast_to(
                    terms_ref[slot * 2 + half, first + 12 : first + 13, :], wide
                ).astype(BF16)
                chosen.append(jnp.where(pick == steps_iota[0], one, zero))
                for part, piece in enumerate(split3(terms_ref[slot * 2 + half, first : first + 16, :])):
                    pieces[part].append(piece.astype(BF16))
            scene_ref[slot, bucket * SUB : (bucket + 1) * SUB, :SCENE_LANES] = lax.dot_general(
                jnp.concatenate(chosen * 3, axis=1),
                jnp.concatenate(pieces[0] + pieces[1] + pieces[2], axis=1),
                (((1,), (1,)), ((), ())),
                preferred_element_type=F32,
            )[:SUB]
        total = scene_ref[slot, pl.ds(0, SUB, stride=SUB), :]
        for scene in range(1, 8):
            value = pltpu.roll(
                scene_ref[slot, pl.ds(scene, SUB, stride=SUB), :], scene * SCENE_LANES, 1
            )
            total = jnp.where(lane // SCENE_LANES == scene, value, total)
        place = pl.ds(group * SUB, SUB)
        total_ref[place, :] = total
        chain = tie_row(group, 8 + CHAIN_SENT // SCENE_LANES)
        chain_lane = (lane // SCENE_LANES) * SCENE_LANES + CHAIN_SENT % SCENE_LANES
        place_ref[place, :] = take_lanes(chain, chain_lane) * 256.0 + take_lanes(
            chain, chain_lane + 1
        )

    def second_pass(step, carry):
        for slot in range(TOGETHER):
            tie_terms(step * TOGETHER + slot, slot)
        for slot in range(TOGETHER):
            scene_sums(step * TOGETHER + slot, slot)
        return carry

    lax.fori_loop(0, groups // TOGETHER, second_pass, 0)

    segment = 4 * LANES
    word = lane % SCENE_LANES
    stacked = []
    for near in range(HALO):
        rows = []
        for strip in range(strips):
            for side in range(2):
                at = float(strip * segment + (near if side else segment - HALO + near))
                for block in range(0, tiles, SUB):
                    here = [pl.ds(s * tiles + block, SUB) for s in range(strips)]
                    rows.append(
                        sum(jnp.where(place_ref[h, :] == at, total_ref[h, :], 0.0) for h in here)
                    )
        stacked.append(jnp.concatenate(rows, axis=0))
    stacked = jnp.concatenate(stacked, axis=1)
    source = sublane_iota((HALO * LANES, 2 * LANES))
    target = lane_iota((HALO * LANES, 2 * LANES))
    chosen = (source % SCENE_LANES == target // SCENE_LANES) & (
        target % SCENE_LANES == source // LANES + POS_LANE + 1
    )
    chosen = jnp.where(chosen, 1.0, 0.0).astype(BF16)
    moved = sum(
        jnp.dot(part.astype(BF16), chosen, preferred_element_type=F32)
        for part in reversed(split3(stacked))
    )
    flag = lane // SCENE_LANES == 4
    for side in range(2):
        for part in range(2):
            for strip in range(strips):
                slot = strip * 4 + side * 2 + part
                edge = tiles if side else SUB
                halo_ref[slot, edge : edge + SUB, :] = jnp.zeros(vreg, F32)
                for block in range(0, tiles, SUB):
                    at = (strip * 2 + side) * tiles + block
                    value = moved[at : at + SUB, part * LANES : (part + 1) * LANES]
                    if part:
                        value = jnp.where(flag, 1.0, value)
                    first = SUB + block + (-1 if side else 1)
                    halo_ref[slot, first : first + SUB, :] = value
    for strip in range(strips):
        start = float(strip * segment)
        for block in range(0, tiles, SUB):
            for source in range(strips):
                place = place_ref[pl.ds(source * tiles + block, SUB), :] - start
                inside = (place >= 0.0) & (place < float(segment))
                value = total_ref[pl.ds(source * tiles + block, SUB), :]
                value = jnp.where(word == POS_LANE, jnp.where(inside, place, -1.0), value)
                value = jnp.where(
                    word > POS_LANE,
                    halo_ref[strip * 4 + source, SUB + block : 2 * SUB + block, :],
                    value,
                )
                out_ref[
                    pl.ds((strip * tiles + block) * strips + source, SUB, stride=strips), :
                ] = value


def chain_kernel(got_ref, out_ref, turned_ref, *, coupling):
    scenes = out_ref.shape[1]
    parts = scenes // 256
    part_rows = 3 * SCENE_LANES
    total = jnp.zeros((parts * part_rows, 256), F32)
    border = jnp.zeros((SUB, LANES), F32)
    for first in range(0, got_ref.shape[0], LANES):
        block = got_ref[first : first + LANES, :]
        for row in range(0, LANES, SUB):
            border = border + block[row : row + SUB]
        turned = block.T
        values = jnp.concatenate(
            [turned[k * SCENE_LANES : (k + 1) * SCENE_LANES] for k in range(8)], axis=1
        )
        position = values[POS_LANE : POS_LANE + 1]
        part_of = (position * (1.0 / 256.0)).astype(I32).astype(F32)
        held = jnp.broadcast_to(part_of, values.shape).astype(BF16)
        pieces = [piece.astype(BF16) for piece in split3(values)]
        zero = jnp.zeros(values.shape, BF16)
        left = [
            jnp.where(held == jnp.full(values.shape, part, BF16), piece, zero)
            for part in range(parts)
            for piece in pieces
        ]
        total = total + lax.dot_general(
            jnp.concatenate(left, axis=0),
            one_hot_rows(position - 256.0 * part_of),
            (((1,), (1,)), ((), ())),
            preferred_element_type=F32,
        )
    sums = jnp.concatenate(
        [
            total[first + 32 : first + 48] + total[first + 16 : first + 32] + total[first : first + 16]
            for first in range(0, parts * part_rows, part_rows)
        ],
        axis=1,
    )
    sums = jnp.where(sublane_iota(sums.shape) == POS_LANE, 1.0, sums)

    border = border + pltpu.roll(border, 4, 0)
    turned_ref[...] = jnp.concatenate([border] * (LANES // SUB), axis=0).T
    lane = lane_iota((SUB, LANES))
    sides = []
    for side in range(2):
        parts = []
        for part in range(2):
            value = jnp.zeros((SUB, LANES), F32)
            for near in range(HALO):
                column = turned_ref[pl.ds(POS_LANE + 1 + near, SUB, stride=SCENE_LANES), :]
                row = side * 2 + part
                here = lane == (near if side else LANES - HALO + near)
                value = jnp.where(here, column[:, row : row + 1], value)
            parts.append(value)
        sides.append(jnp.concatenate(parts, axis=0))
    sums = jnp.concatenate([sides[0], sums, sides[1]], axis=1)
    width = sums.shape[1]
    rows = [sums[row : row + 1] for row in range(13)]
    matrix = [
        rows[0] + 2.0 * coupling,
        rows[1],
        rows[2],
        rows[3] + 2.0 * coupling,
        rows[4],
        rows[5] + 2.0 * coupling,
    ]
    exists = rows[POS_LANE] > 0.0
    inverse = [jnp.where(exists, entry, 0.0) for entry in inverse_sym(matrix)]

    def apply_pair(vectors):
        return apply_sym(inverse, *vectors[:3]) + apply_sym(inverse, *vectors[3:])

    right_sides = rows[6:12]
    smoothed = apply_pair(right_sides)
    for _ in range(SWEEPS - 1):
        smoothed = apply_pair(
            [
                side + coupling * (pltpu.roll(value, 1, 1) + pltpu.roll(value, width - 1, 1))
                for side, value in zip(right_sides, smoothed)
            ]
        )
    for row in range(6):
        out_ref[row : row + 1, :] = smoothed[row][:, LANES : LANES + scenes]


def call(kernel, out_shape, scratch=(), name=None, vmem=48, **specs):
    return pl.pallas_call(
        kernel,
        out_shape=out_shape,
        scratch_shapes=list(scratch),
        compiler_params=pltpu.CompilerParams(vmem_limit_bytes=vmem * 1024 * 1024),
        name=name,
        **specs,
    )


def shape(dims, dtype=F32):
    return jax.ShapeDtypeStruct(dims, dtype)


def tile_call(got, ground, strips):
    owners = got.shape[0] // BUCKET_ROWS
    tie_rows = owners * 2
    points = ground.shape[1]
    return call(
        functools.partial(tile_kernel, strips=strips),
        (shape(ground.shape), shape((owners * strips, LANES))),
        [
            pltpu.VMEM((9, tie_rows, LANES), F32),
            pltpu.VMEM((SUB * BUCKET_PARTS, LANES), F32),
            pltpu.VMEM((SUB * BUCKET_PARTS, LANES), F32),
            pltpu.VMEM((2, SUB * PART_ROWS, LANES), F32),
            pltpu.VMEM((3 * points // LANES * SUB, LANES), F32),
            pltpu.VMEM((3 * points // LANES, LANES), F32),
            pltpu.VMEM((owners, LANES), F32),
            pltpu.VMEM((owners, LANES), F32),
            pltpu.VMEM((strips * 4, owners // strips + 2 * SUB, LANES), F32),
            pltpu.VMEM((SCENE_ROWS * SCENE_LANES * SUB, LANES), F32),
            pltpu.VMEM((2 * TOGETHER, SUB * TERM_ROWS, LANES), F32),
            pltpu.VMEM((TOGETHER, SUB * SUB, LANES), F32),
        ],
        name="tile_sums",
    )(got, ground)


def per_device(
    num_coef,
    den_coef,
    bias,
    scene_chain,
    bucket_scenes,
    tie_counts,
    tie_obs,
    tie_prior,
    tie_pick,
    tie_point,
    ground,
):
    strips = lax.axis_size("strip")
    tiles = lax.axis_size("tile")
    owners = strips * tiles
    tie_dev = tie_prior.shape[0]
    tie_rows = tie_dev // LANES
    scenes_dev = num_coef.shape[1]
    coupling = smooth_gain * (tie_dev // scenes_dev)

    arguments = [
        num_coef,
        den_coef,
        bias,
        scene_chain.reshape(1, scenes_dev),
        bucket_scenes,
        tie_counts,
        tie_obs.reshape(2, tie_rows, LANES).transpose(1, 0, 2).reshape(2 * tie_rows, LANES),
        tie_prior.reshape(tie_rows, LANES),
        tie_pick.reshape(tie_rows, LANES),
        tie_point.reshape(tie_rows, LANES),
    ]
    sent = call(
        pack_kernel,
        shape((owners * BUCKET_ROWS, LANES)),
        [pltpu.VMEM(argument.shape, argument.dtype) for argument in arguments]
        + [
            pltpu.VMEM((CHAIN_ROW + SUB, scenes_dev), F32),
            pltpu.SemaphoreType.DMA((len(arguments),)),
        ],
        name="pack",
        vmem=64,
        in_specs=[pl.BlockSpec(memory_space=pltpu.HBM)] * len(arguments),
    )(*arguments)
    got = lax.all_to_all(
        sent.reshape(owners, BUCKET_ROWS // 2, 2, LANES), AXES, 0, 0, tiled=True
    ).reshape(owners * BUCKET_ROWS, LANES)
    ground_next, totals = tile_call(got, ground, strips)
    got_totals = lax.all_to_all(totals.reshape(owners, strips, LANES), AXES, 0, 0, tiled=True)
    smoothed = call(
        functools.partial(chain_kernel, coupling=coupling),
        shape((6, scenes_dev)),
        [pltpu.VMEM((LANES, LANES), F32)],
        name="chain",
    )(got_totals.reshape(owners * strips, LANES))
    return ground_next, smoothed


def solution(mesh):
    in_specs = (
        P(None, AXES),
        P(None, AXES),
        P(None, AXES),
        P(AXES),
        P(AXES, None),
        P(AXES, None),
        P(None, AXES),
        P(AXES),
        P(AXES),
        P(AXES),
        P(None, AXES),
    )
    out_specs = (P(None, AXES), P(None, AXES))
    return jax.shard_map(
        per_device, mesh=mesh, in_specs=in_specs, out_specs=out_specs, check_vma=False
    )
```

```python
import functools

import jax
import jax.numpy as jnp
from jax import lax
from jax.experimental import pallas as pl
from jax.experimental.pallas import tpu as pltpu
from jax.sharding import PartitionSpec as P

SWEEPS = 4
AXES = ("strip", "tile")
F32 = jnp.float32
BF16 = jnp.bfloat16
I32 = jnp.int32
LANES = 128
SUB = 8

cauchy_scale = 1.0
point_damping = 1.0
smooth_gain = 0.25

LATE_TERMS = 64
BIAS_ROW = 80
CHAIN_ROW = 104
CHAIN_SENT = 88
SCENE_ROWS = 6
LANE_STEP = 2
BUCKET_ROWS = 8 + SCENE_ROWS
SCENE_LANES = 16
POS_LANE = 12
TOGETHER = 16
BUFFERS = 2
HALO = SWEEPS - 1
PART_ROWS = 32
SUM_ROWS = 36
TERM_ROWS = 20
BUCKET_PARTS = 68


def lane_iota(shape):
    return lax.broadcasted_iota(I32, shape, len(shape) - 1)


def sublane_iota(shape):
    return lax.broadcasted_iota(I32, shape, len(shape) - 2)


def split3(value):
    high = value.astype(BF16).astype(F32)
    rest = value - high
    middle = rest.astype(BF16).astype(F32)
    return high, middle, rest - middle


def one_hot_rows(low):
    wide = (16, low.shape[1])
    held = jnp.broadcast_to(low, wide).astype(BF16)
    one = jnp.ones(wide, BF16)
    zero = jnp.zeros(wide, BF16)
    rows = sublane_iota(wide)
    return jnp.concatenate(
        [
            jnp.where(held == (rows + first).astype(F32).astype(BF16), one, zero)
            for first in range(0, 256, 16)
        ],
        axis=0,
    )


def take_lanes(table, lanes):
    return jnp.take_along_axis(table, lanes, axis=1, mode="promise_in_bounds")


def inverse_sym(matrix):
    cofactor = [
        matrix[3] * matrix[5] - matrix[4] * matrix[4],
        matrix[2] * matrix[4] - matrix[1] * matrix[5],
        matrix[1] * matrix[4] - matrix[2] * matrix[3],
        matrix[0] * matrix[5] - matrix[2] * matrix[2],
        matrix[1] * matrix[2] - matrix[0] * matrix[4],
        matrix[0] * matrix[3] - matrix[1] * matrix[1],
    ]
    determinant = matrix[0] * cofactor[0] + matrix[1] * cofactor[1] + matrix[2] * cofactor[2]
    return [cofactor_entry / determinant for cofactor_entry in cofactor]


def apply_sym(inverse, comp_one, comp_two, comp_three):
    return [
        inverse[0] * comp_one + inverse[1] * comp_two + inverse[2] * comp_three,
        inverse[1] * comp_one + inverse[3] * comp_two + inverse[4] * comp_three,
        inverse[2] * comp_one + inverse[4] * comp_two + inverse[5] * comp_three,
    ]


def pack_kernel(
    num_hbm,
    den_hbm,
    bias_hbm,
    chain_hbm,
    list_hbm,
    counts_hbm,
    obs_hbm,
    prior_hbm,
    pick_hbm,
    point_hbm,
    out_ref,
    num_ref,
    den_ref,
    bias_ref,
    chain_ref,
    list_ref,
    counts_ref,
    obs_ref,
    prior_ref,
    pick_ref,
    point_ref,
    table_ref,
    sems,
):
    copies = [
        pltpu.make_async_copy(source, target, sems.at[index])
        for index, (source, target) in enumerate(
            [
                (num_hbm, num_ref),
                (den_hbm, den_ref),
                (bias_hbm, bias_ref),
                (chain_hbm, chain_ref),
                (list_hbm, list_ref),
                (counts_hbm, counts_ref),
                (obs_hbm, obs_ref),
                (prior_hbm, prior_ref),
                (pick_hbm, pick_ref),
                (point_hbm, point_ref),
            ]
        )
    ]
    for copy in copies:
        copy.start()
    owners = out_ref.shape[0] // BUCKET_ROWS
    scenes = num_ref.shape[1]
    listed = list_ref.shape[1]
    table_ref[...] = jnp.zeros(table_ref.shape, F32)
    for copy in copies[:5]:
        copy.wait()
    numer = num_ref[...].astype(F32)
    denom = den_ref[...].astype(F32)
    for which in range(2):
        table_ref[16 * which : 16 * which + 16, :] = numer[20 * which : 20 * which + 16]
        table_ref[33 + 16 * which : 48 + 16 * which, :] = denom[19 * which : 19 * which + 15]
        late = LATE_TERMS + 4 * which
        table_ref[late : late + 4, :] = numer[20 * which + 16 : 20 * which + 20]
        table_ref[late + 8 : late + 12, :] = denom[19 * which + 15 : 19 * which + 19]
    for part, value in enumerate(split3(bias_ref[...])):
        first = BIAS_ROW + part * SUB
        table_ref[first : first + 6, :] = value
    place = (chain_ref[...] & (scenes - 1)) + (lane_iota((1, scenes)) // (scenes // 4)) * scenes
    table_ref[CHAIN_ROW : CHAIN_ROW + 1, :] = (place >> 8).astype(F32)
    table_ref[CHAIN_ROW + 1 : CHAIN_ROW + 2, :] = (place & 255).astype(F32)
    table = table_ref[...].astype(BF16)
    lane = lane_iota((SUB, LANES))
    per_row = LANES // SUB
    index = (lane % per_row) * SUB + sublane_iota((SUB, LANES))
    lists = jnp.zeros((SUB, LANES), F32)
    for row in range(listed // LANES):
        ids = list_ref[:, row * LANES : (row + 1) * LANES].astype(F32)
        found = take_lanes(jnp.broadcast_to(ids, (SUB, LANES)), index)
        lists = jnp.where(lane // per_row == row, found, lists)
    lows = []
    for first in range(0, scenes, 256):
        inside = (lists >= float(first)) & (lists < float(first + 256))
        lows.append(jnp.where(inside, lists - float(first), -1.0))
    got = []
    for pair in range(0, SUB, 2):
        onehot = []
        for k in (pair, pair + 1):
            onehot.append(
                jnp.concatenate([one_hot_rows(low[k : k + 1]) for low in lows], axis=0)
            )
        both = jnp.dot(
            table, jnp.concatenate(onehot, axis=1), preferred_element_type=F32
        )
        for part in range(0, 256, LANES):
            one = both[:, part : part + LANES]
            bias_rows = (
                one[BIAS_ROW : BIAS_ROW + SUB]
                + one[BIAS_ROW + SUB : BIAS_ROW + 2 * SUB]
                + one[BIAS_ROW + 2 * SUB : BIAS_ROW + 3 * SUB]
            )
            got.append(jnp.concatenate([one[:BIAS_ROW], bias_rows, one[CHAIN_ROW:]], axis=0))
    for block in range(SCENE_ROWS):
        words = slice(block * SCENE_LANES, (block + 1) * SCENE_LANES)
        turned = jnp.concatenate([one[words] for one in got], axis=0).T
        for group in range(owners // SUB):
            out_ref[
                pl.ds(group * SUB * BUCKET_ROWS + 8 + block, SUB, stride=BUCKET_ROWS), :
            ] = turned[group * SUB : (group + 1) * SUB]
    for copy in copies[5:]:
        copy.wait()
    counts = jnp.broadcast_to(counts_ref[...].astype(F32), (owners, owners)).T
    slot = lane.astype(F32)
    for group in range(owners // SUB):
        live_count = counts[group * SUB : (group + 1) * SUB, :1]
        base = group * SUB * BUCKET_ROWS

        def put(row, value):
            out_ref[pl.ds(base + row, SUB, stride=BUCKET_ROWS), :] = value

        for row in range(4):
            put(row, obs_ref[pl.ds(group * SUB * 4 + row, SUB, stride=4), :])
        for half in range(2):
            rows = pl.ds(group * SUB * 2 + half, SUB, stride=2)
            live = slot + float(half * LANES) < live_count
            put(4 + half, jnp.where(live, prior_ref[rows, :], 0.0))
            put(6 + half, (pick_ref[rows, :] * 2048 + point_ref[rows, :]).astype(F32))


def ratios(coef, east, north, up):
    east_sq, north_sq, up_sq = east * east, north * north, up * up
    east_north, east_up, north_up = east * north, east * up, north * up
    terms = [
        (1, None, None, None),
        (east, 1, None, None),
        (north, None, 1, None),
        (up, None, None, 1),
        (east_north, north, east, None),
        (east_up, up, None, east),
        (north_up, None, up, north),
        (east_sq, 2.0 * east, None, None),
        (north_sq, None, 2.0 * north, None),
        (up_sq, None, None, 2.0 * up),
        (east_north * up, north_up, east_up, east_north),
        (east_sq * east, 3.0 * east_sq, None, None),
        (east * north_sq, north_sq, 2.0 * east_north, None),
        (east * up_sq, up_sq, None, 2.0 * east_up),
        (east_sq * north, 2.0 * east_north, east_sq, None),
        (north_sq * north, None, 3.0 * north_sq, None),
        (north * up_sq, None, up_sq, 2.0 * north_up),
        (east_sq * up, 2.0 * east_up, None, east_sq),
        (north_sq * up, None, 2.0 * north_up, north_sq),
        (up_sq * up, None, None, 3.0 * up_sq),
    ]
    sums = [[None] * 4 for _ in range(4)]
    for cubic in (2, 3):
        sums[cubic][0] = jnp.ones_like(east)

    def add(cubic, term, row):
        if cubic >= 2 and term == 0:
            return
        value = coef(row)
        for which, factor in enumerate(terms[term]):
            if factor is None:
                continue
            product = value if isinstance(factor, int) else value * factor
            held = sums[cubic][which]
            sums[cubic][which] = product if held is None else held + product

    words = [w for first in range(LANE_STEP) for w in range(first, SCENE_LANES, LANE_STEP)]
    bias = [None] * 6
    for word in words:
        for cubic in range(4):
            add(cubic, word, cubic * SCENE_LANES + word)
        add(word // 4, 16 + word % 4, LATE_TERMS + word)
        if word < 6:
            bias[word] = coef(BIAS_ROW + word)
    found = []
    for top, bottom in ((sums[0], sums[2]), (sums[1], sums[3])):
        quotient = top[0] / bottom[0]
        found.append(quotient)
        found.append(
            [(top[which] - quotient * bottom[which]) / bottom[0] for which in range(1, 4)]
        )
    return found, bias


def tile_kernel(
    got_ref,
    ground_ref,
    next_ref,
    out_ref,
    packed_ref,
    parts_ref,
    sums_ref,
    table_ref,
    step_ref,
    total_ref,
    place_ref,
    halo_ref,
    coef_ref,
    terms_ref,
    scene_ref,
    *,
    strips,
):
    owners = got_ref.shape[0] // BUCKET_ROWS
    groups = owners // SUB
    tiles = owners // strips
    points = ground_ref.shape[1]
    point_rows = points // LANES
    vreg = (SUB, LANES)
    lane = lane_iota(vreg)

    def fill_table(value):
        for axis in range(3):
            for row in range(point_rows):
                at = (axis * point_rows + row) * SUB
                table_ref[at : at + SUB, :] = jnp.broadcast_to(value(axis, row), vreg)

    fill_table(lambda axis, row: ground_ref[axis : axis + 1, row * LANES : (row + 1) * LANES])

    def tie_row(group, row):
        return got_ref[pl.ds(group * (SUB * BUCKET_ROWS) + row, SUB, stride=BUCKET_ROWS), :]

    def code_of(group, half):
        code = tie_row(group, 6 + half).astype(I32)
        return code >> 11, code & (points - 1)

    def gather_points(point):
        high = point >> 7
        low = point & (LANES - 1)
        found = [None] * 3
        for row in range(point_rows):
            here = high == row
            for axis in range(3):
                at = (axis * point_rows + row) * SUB
                value = take_lanes(table_ref[at : at + SUB, :], low)
                found[axis] = value if row == 0 else jnp.where(here, value, found[axis])
        return found

    def turn_scenes(group):
        for block in range(SCENE_ROWS):
            value = tie_row(group, 8 + block)
            for word in range(0, SCENE_LANES if block < 5 else 6, LANE_STEP):
                at = (block * SCENE_LANES + word) * SUB
                coef_ref[group % BUFFERS, at : at + SUB, :] = (
                    pltpu.roll(value, LANES - word, 1) if word else value
                )

    def first_pass(group, half):
        pick, point = code_of(group, half)
        first_lane = pick * SCENE_LANES
        east, north, up = gather_points(point)

        def coef(row):
            at = (row - row % LANE_STEP) * SUB
            return take_lanes(
                coef_ref[group % BUFFERS, at : at + SUB, :], first_lane + row % LANE_STEP
            )

        line_obs = tie_row(group, 2 * half)
        samp_obs = tie_row(group, 2 * half + 1)
        prior = tie_row(group, 4 + half)
        (line_ratio, line_jac, samp_ratio, samp_jac), bias = ratios(coef, east, north, up)
        line_res = line_obs - (line_ratio + bias[0] + bias[1] * samp_obs + bias[2] * line_obs)
        samp_res = samp_obs - (samp_ratio + bias[3] + bias[4] * samp_obs + bias[5] * line_obs)
        weight = prior / (1.0 + (line_res * line_res + samp_res * samp_res) / cauchy_scale)
        place = pl.ds((group * 2 + half) * SUB, SUB)
        for row, value in enumerate([line_res, samp_res] + line_jac + samp_jac + [weight]):
            packed_ref[row, place, :] = value
        pairs = [(0, 0), (0, 1), (0, 2), (1, 1), (1, 2), (2, 2)]
        sums = [weight * (line_jac[a] * line_jac[b] + samp_jac[a] * samp_jac[b]) for a, b in pairs]
        sums += [weight * (line_jac[a] * line_res + samp_jac[a] * samp_res) for a in range(3)]

        def put(row, value):
            parts_ref[
                group % BUFFERS, pl.ds(half * PART_ROWS + row, SUB, stride=BUCKET_PARTS), :
            ] = value

        for row, value in enumerate(sums):
            for part, piece in enumerate(split3(value)):
                put(row * 3 + part, piece)
        put(27, (point >> 8).astype(F32))
        put(28, (point & 255).astype(F32))

    wide = (16, LANES)
    steps_iota = [
        (sublane_iota(wide) + 16 * row).astype(F32).astype(BF16) for row in range(16)
    ]
    one = jnp.ones(wide, BF16)
    zero = jnp.zeros(wide, BF16)

    def product_of(group, first_bucket, count):
        held = parts_ref.at[group % BUFFERS]
        left = []
        right = []
        for bucket in range(first_bucket, first_bucket + count):
            for half in range(2):
                first = bucket * BUCKET_PARTS + half * PART_ROWS
                values = held[first : first + PART_ROWS, :].astype(BF16)
                high = jnp.broadcast_to(held[first + 27 : first + 28, :], wide).astype(BF16)
                low = jnp.broadcast_to(held[first + 28 : first + 29, :], wide).astype(BF16)
                rows = []
                for index in range(8):
                    here = high == jnp.full(wide, index, BF16)
                    rows.append(jnp.where(here, values[:16], zero))
                    rows.append(jnp.where(here, values[16:], zero))
                left.append(jnp.concatenate(rows, axis=0))
                right.append(
                    jnp.concatenate(
                        [jnp.where(low == step, one, zero) for step in steps_iota], axis=0
                    )
                )
        return lax.dot_general(
            jnp.concatenate(left, axis=1),
            jnp.concatenate(right, axis=1),
            (((1,), (1,)), ((), ())),
            preferred_element_type=F32,
        )

    def sum_pass(group, first_bucket, count):
        products = [
            product_of(group, first_bucket + part * count // 2, count // 2)
            for part in range(2)
        ]
        product = products[0] + products[1]
        for half in range(2):
            for index in range(SUB):
                held = slice(index * SUM_ROWS, index * SUM_ROWS + PART_ROWS)
                rows = slice(index * PART_ROWS, (index + 1) * PART_ROWS)
                sums_ref[half, held, :] += product[rows, half * LANES : (half + 1) * LANES]

    sums_ref[...] = jnp.zeros(sums_ref.shape, F32)
    for group in range(groups + 1):
        if group < groups:
            turn_scenes(group)
        if group:
            sum_pass(group - 1, 0, SUB)
        if group < groups:
            for half in range(2):
                first_pass(group, half)

    def point_sum(row, half):
        return sum(
            sums_ref[half, pl.ds(row * 3 + part, SUB, stride=SUM_ROWS), :] for part in (2, 1, 0)
        )

    for half in range(2):
        sums = [point_sum(row, half) for row in range(9)]
        matrix = [
            sums[0] + point_damping,
            sums[1],
            sums[2],
            sums[3] + point_damping,
            sums[4],
            sums[5] + point_damping,
        ]
        steps = apply_sym(inverse_sym(matrix), sums[6], sums[7], sums[8])
        for axis in range(3):
            step_ref[pl.ds(axis * point_rows + half, SUB, stride=2), :] = steps[axis]
    for axis in range(3):
        for row in range(point_rows):
            columns = slice(row * LANES, (row + 1) * LANES)
            at = axis * point_rows + row
            next_ref[axis : axis + 1, columns] = (
                ground_ref[axis : axis + 1, columns] + step_ref[at : at + 1, :]
            )
    fill_table(
        lambda axis, row: step_ref[axis * point_rows + row : axis * point_rows + row + 1, :]
    )

    def tie_terms(group, slot):
        rows = []
        picks = []
        for half in range(2):
            pick, point = code_of(group, half)
            tie_step = gather_points(point)
            place = pl.ds((group * 2 + half) * SUB, SUB)
            packed = [packed_ref[row, place, :] for row in range(9)]
            line_obs = tie_row(group, 2 * half)
            samp_obs = tie_row(group, 2 * half + 1)
            weight = packed[8]
            line_res = packed[0] - (
                packed[2] * tie_step[0] + packed[3] * tie_step[1] + packed[4] * tie_step[2]
            )
            samp_res = packed[1] - (
                packed[5] * tie_step[0] + packed[6] * tie_step[1] + packed[7] * tie_step[2]
            )
            samp_weight = weight * samp_obs
            line_weight = weight * line_obs
            rows.append(
                [
                    weight,
                    samp_weight,
                    line_weight,
                    samp_weight * samp_obs,
                    samp_weight * line_obs,
                    line_weight * line_obs,
                    weight * line_res,
                    samp_weight * line_res,
                    line_weight * line_res,
                    weight * samp_res,
                    samp_weight * samp_res,
                    line_weight * samp_res,
                ]
            )
            picks.append(pick)
        for half in range(2):
            spare = [jnp.zeros(vreg, F32)] * 3
            for row, value in enumerate(rows[half] + [picks[half].astype(F32)] + spare):
                terms_ref[slot * 2 + half, pl.ds(row, SUB, stride=TERM_ROWS), :] = value

    def scene_sums(group, slot):
        for bucket in range(SUB):
            chosen = []
            pieces = [[], [], []]
            for half in range(2):
                first = bucket * TERM_ROWS
                pick = jnp.broadcast_to(
                    terms_ref[slot * 2 + half, first + 12 : first + 13, :], wide
                ).astype(BF16)
                chosen.append(jnp.where(pick == steps_iota[0], one, zero))
                for part, piece in enumerate(split3(terms_ref[slot * 2 + half, first : first + 16, :])):
                    pieces[part].append(piece.astype(BF16))
            scene_ref[slot, bucket * SUB : (bucket + 1) * SUB, :SCENE_LANES] = lax.dot_general(
                jnp.concatenate(chosen * 3, axis=1),
                jnp.concatenate(pieces[0] + pieces[1] + pieces[2], axis=1),
                (((1,), (1,)), ((), ())),
                preferred_element_type=F32,
            )[:SUB]
        total = scene_ref[slot, pl.ds(0, SUB, stride=SUB), :]
        for scene in range(1, 8):
            value = pltpu.roll(
                scene_ref[slot, pl.ds(scene, SUB, stride=SUB), :], scene * SCENE_LANES, 1
            )
            total = jnp.where(lane // SCENE_LANES == scene, value, total)
        place = pl.ds(group * SUB, SUB)
        total_ref[place, :] = total
        chain = tie_row(group, 8 + CHAIN_SENT // SCENE_LANES)
        chain_lane = (lane // SCENE_LANES) * SCENE_LANES + CHAIN_SENT % SCENE_LANES
        place_ref[place, :] = take_lanes(chain, chain_lane) * 256.0 + take_lanes(
            chain, chain_lane + 1
        )

    def second_pass(step, carry):
        for slot in range(TOGETHER):
            tie_terms(step * TOGETHER + slot, slot)
        for slot in range(TOGETHER):
            scene_sums(step * TOGETHER + slot, slot)
        return carry

    lax.fori_loop(0, groups // TOGETHER, second_pass, 0)

    segment = 4 * LANES
    word = lane % SCENE_LANES
    stacked = []
    for near in range(HALO):
        rows = []
        for strip in range(strips):
            for side in range(2):
                at = float(strip * segment + (near if side else segment - HALO + near))
                for block in range(0, tiles, SUB):
                    here = [pl.ds(s * tiles + block, SUB) for s in range(strips)]
                    rows.append(
                        sum(jnp.where(place_ref[h, :] == at, total_ref[h, :], 0.0) for h in here)
                    )
        stacked.append(jnp.concatenate(rows, axis=0))
    stacked = jnp.concatenate(stacked, axis=1)
    source = sublane_iota((HALO * LANES, 2 * LANES))
    target = lane_iota((HALO * LANES, 2 * LANES))
    chosen = (source % SCENE_LANES == target // SCENE_LANES) & (
        target % SCENE_LANES == source // LANES + POS_LANE + 1
    )
    chosen = jnp.where(chosen, 1.0, 0.0).astype(BF16)
    moved = sum(
        jnp.dot(part.astype(BF16), chosen, preferred_element_type=F32)
        for part in reversed(split3(stacked))
    )
    flag = lane // SCENE_LANES == 4
    for side in range(2):
        for part in range(2):
            for strip in range(strips):
                slot = strip * 4 + side * 2 + part
                edge = tiles if side else SUB
                halo_ref[slot, edge : edge + SUB, :] = jnp.zeros(vreg, F32)
                for block in range(0, tiles, SUB):
                    at = (strip * 2 + side) * tiles + block
                    value = moved[at : at + SUB, part * LANES : (part + 1) * LANES]
                    if part:
                        value = jnp.where(flag, 1.0, value)
                    first = SUB + block + (-1 if side else 1)
                    halo_ref[slot, first : first + SUB, :] = value
    for strip in range(strips):
        start = float(strip * segment)
        for block in range(0, tiles, SUB):
            for source in range(strips):
                place = place_ref[pl.ds(source * tiles + block, SUB), :] - start
                inside = (place >= 0.0) & (place < float(segment))
                value = total_ref[pl.ds(source * tiles + block, SUB), :]
                value = jnp.where(word == POS_LANE, jnp.where(inside, place, -1.0), value)
                value = jnp.where(
                    word > POS_LANE,
                    halo_ref[strip * 4 + source, SUB + block : 2 * SUB + block, :],
                    value,
                )
                out_ref[
                    pl.ds((strip * tiles + block) * strips + source, SUB, stride=strips), :
                ] = value


def chain_kernel(got_ref, out_ref, turned_ref, joined_ref, *, coupling):
    scenes = out_ref.shape[1]
    parts = scenes // 256
    part_rows = 3 * SCENE_LANES
    total = jnp.zeros((parts * part_rows, 256), F32)
    border = jnp.zeros((SUB, LANES), F32)
    for first in range(0, got_ref.shape[0], LANES):
        block = got_ref[first : first + LANES, :]
        for row in range(0, LANES, SUB):
            border = border + block[row : row + SUB]
        turned = block.T
        values = jnp.concatenate(
            [turned[k * SCENE_LANES : (k + 1) * SCENE_LANES] for k in range(8)], axis=1
        )
        position = values[POS_LANE : POS_LANE + 1]
        part_of = (position * (1.0 / 256.0)).astype(I32).astype(F32)
        held = jnp.broadcast_to(part_of, values.shape).astype(BF16)
        pieces = [piece.astype(BF16) for piece in split3(values)]
        zero = jnp.zeros(values.shape, BF16)
        left = [
            jnp.where(held == jnp.full(values.shape, part, BF16), piece, zero)
            for part in range(parts)
            for piece in pieces
        ]
        total = total + lax.dot_general(
            jnp.concatenate(left, axis=0),
            one_hot_rows(position - 256.0 * part_of),
            (((1,), (1,)), ((), ())),
            preferred_element_type=F32,
        )
    sums = jnp.concatenate(
        [
            total[first + 32 : first + 48] + total[first + 16 : first + 32] + total[first : first + 16]
            for first in range(0, parts * part_rows, part_rows)
        ],
        axis=1,
    )
    sums = jnp.where(sublane_iota(sums.shape) == POS_LANE, 1.0, sums)

    border = border + pltpu.roll(border, 4, 0)
    turned_ref[...] = jnp.concatenate([border] * (LANES // SUB), axis=0).T
    lane = lane_iota((SUB, LANES))
    sides = []
    for side in range(2):
        parts = []
        for part in range(2):
            value = jnp.zeros((SUB, LANES), F32)
            for near in range(HALO):
                column = turned_ref[pl.ds(POS_LANE + 1 + near, SUB, stride=SCENE_LANES), :]
                row = side * 2 + part
                here = lane == (near if side else LANES - HALO + near)
                value = jnp.where(here, column[:, row : row + 1], value)
            parts.append(value)
        sides.append(jnp.concatenate(parts, axis=0))
    sums = jnp.concatenate([sides[0], sums, sides[1]], axis=1)
    width = sums.shape[1]
    joined_ref[...] = sums
    rows = [joined_ref[row : row + 1, :] for row in range(6)]
    matrix = [
        rows[0] + 2.0 * coupling,
        rows[1],
        rows[2],
        rows[3] + 2.0 * coupling,
        rows[4],
        rows[5] + 2.0 * coupling,
    ]
    exists = joined_ref[POS_LANE : POS_LANE + 1, :] > 0.0
    inverse = [
        jnp.broadcast_to(jnp.where(exists, entry, 0.0), (2, width))
        for entry in inverse_sym(matrix)
    ]
    right_sides = [
        jnp.concatenate(
            [joined_ref[6 + term : 7 + term, :], joined_ref[9 + term : 10 + term, :]], axis=0
        )
        for term in range(3)
    ]
    smoothed = apply_sym(inverse, *right_sides)
    for _ in range(SWEEPS - 1):
        smoothed = apply_sym(
            inverse,
            *[
                side + coupling * (pltpu.roll(value, 1, 1) + pltpu.roll(value, width - 1, 1))
                for side, value in zip(right_sides, smoothed)
            ],
        )
    for term in range(3):
        for row in range(2):
            out_ref[3 * row + term : 3 * row + term + 1, :] = smoothed[term][
                row : row + 1, LANES : LANES + scenes
            ]


def call(kernel, out_shape, scratch=(), name=None, vmem=48, **specs):
    return pl.pallas_call(
        kernel,
        out_shape=out_shape,
        scratch_shapes=list(scratch),
        compiler_params=pltpu.CompilerParams(vmem_limit_bytes=vmem * 1024 * 1024),
        name=name,
        **specs,
    )


def shape(dims, dtype=F32):
    return jax.ShapeDtypeStruct(dims, dtype)


def tile_call(got, ground, strips):
    owners = got.shape[0] // BUCKET_ROWS
    tie_rows = owners * 2
    points = ground.shape[1]
    return call(
        functools.partial(tile_kernel, strips=strips),
        (shape(ground.shape), shape((owners * strips, LANES))),
        [
            pltpu.VMEM((9, tie_rows, LANES), F32),
            pltpu.VMEM((BUFFERS, SUB * BUCKET_PARTS, LANES), F32),
            pltpu.VMEM((2, SUB * SUM_ROWS, LANES), F32),
            pltpu.VMEM((3 * points // LANES * SUB, LANES), F32),
            pltpu.VMEM((3 * points // LANES, LANES), F32),
            pltpu.VMEM((owners, LANES), F32),
            pltpu.VMEM((owners, LANES), F32),
            pltpu.VMEM((strips * 4, owners // strips + 2 * SUB, LANES), F32),
            pltpu.VMEM((BUFFERS, SCENE_ROWS * SCENE_LANES * SUB, LANES), F32),
            pltpu.VMEM((2 * TOGETHER, SUB * TERM_ROWS, LANES), F32),
            pltpu.VMEM((TOGETHER, SUB * SUB, LANES), F32),
        ],
        name="tile_sums",
    )(got, ground)


def per_device(
    num_coef,
    den_coef,
    bias,
    scene_chain,
    bucket_scenes,
    tie_counts,
    tie_obs,
    tie_prior,
    tie_pick,
    tie_point,
    ground,
):
    strips = lax.axis_size("strip")
    tiles = lax.axis_size("tile")
    owners = strips * tiles
    tie_dev = tie_prior.shape[0]
    tie_rows = tie_dev // LANES
    scenes_dev = num_coef.shape[1]
    coupling = smooth_gain * (tie_dev // scenes_dev)

    arguments = [
        num_coef,
        den_coef,
        bias,
        scene_chain.reshape(1, scenes_dev),
        bucket_scenes,
        tie_counts,
        tie_obs.reshape(2, tie_rows, LANES).transpose(1, 0, 2).reshape(2 * tie_rows, LANES),
        tie_prior.reshape(tie_rows, LANES),
        tie_pick.reshape(tie_rows, LANES),
        tie_point.reshape(tie_rows, LANES),
    ]
    sent = call(
        pack_kernel,
        shape((owners * BUCKET_ROWS, LANES)),
        [pltpu.VMEM(argument.shape, argument.dtype) for argument in arguments]
        + [
            pltpu.VMEM((CHAIN_ROW + SUB, scenes_dev), F32),
            pltpu.SemaphoreType.DMA((len(arguments),)),
        ],
        name="pack",
        vmem=64,
        in_specs=[pl.BlockSpec(memory_space=pltpu.HBM)] * len(arguments),
    )(*arguments)
    got = lax.all_to_all(
        sent.reshape(owners, BUCKET_ROWS // 2, 2, LANES), AXES, 0, 0, tiled=True
    ).reshape(owners * BUCKET_ROWS, LANES)
    ground_next, totals = tile_call(got, ground, strips)
    got_totals = lax.all_to_all(totals.reshape(owners, strips, LANES), AXES, 0, 0, tiled=True)
    smoothed = call(
        functools.partial(chain_kernel, coupling=coupling),
        shape((6, scenes_dev)),
        [pltpu.VMEM((LANES, LANES), F32), pltpu.VMEM((16, scenes_dev + 2 * LANES), F32)],
        name="chain",
    )(got_totals.reshape(owners * strips, LANES))
    return ground_next, smoothed


def solution(mesh):
    in_specs = (
        P(None, AXES),
        P(None, AXES),
        P(None, AXES),
        P(AXES),
        P(AXES, None),
        P(AXES, None),
        P(None, AXES),
        P(AXES),
        P(AXES),
        P(AXES),
        P(None, AXES),
    )
    out_specs = (P(None, AXES), P(None, AXES))
    return jax.shard_map(
        per_device, mesh=mesh, in_specs=in_specs, out_specs=out_specs, check_vma=False
    )
```

```python
import functools

import jax
import jax.numpy as jnp
from jax import lax
from jax.experimental import pallas as pl
from jax.experimental.pallas import tpu as pltpu
from jax.sharding import PartitionSpec as P

SWEEPS = 4
AXES = ("strip", "tile")
F32 = jnp.float32
BF16 = jnp.bfloat16
I32 = jnp.int32
LANES = 128
SUB = 8

cauchy_scale = 1.0
point_damping = 1.0
smooth_gain = 0.25

LATE_TERMS = 64
BIAS_ROW = 80
CHAIN_ROW = 104
CHAIN_SENT = 88
SCENE_ROWS = 6
LANE_STEP = 2
BUCKET_ROWS = 8 + SCENE_ROWS
SCENE_LANES = 16
POS_LANE = 12
TOGETHER = 16
BUFFERS = 2
HALO = SWEEPS - 1
PART_ROWS = 32
SUM_ROWS = 36
TERM_ROWS = 20
BUCKET_PARTS = 68


def lane_iota(shape):
    return lax.broadcasted_iota(I32, shape, len(shape) - 1)


def sublane_iota(shape):
    return lax.broadcasted_iota(I32, shape, len(shape) - 2)


def split3(value):
    high = value.astype(BF16).astype(F32)
    rest = value - high
    middle = rest.astype(BF16).astype(F32)
    return high, middle, rest - middle


def one_hot_rows(low):
    wide = (16, low.shape[1])
    held = jnp.broadcast_to(low, wide).astype(BF16)
    one = jnp.ones(wide, BF16)
    zero = jnp.zeros(wide, BF16)
    rows = sublane_iota(wide)
    return jnp.concatenate(
        [
            jnp.where(held == (rows + first).astype(F32).astype(BF16), one, zero)
            for first in range(0, 256, 16)
        ],
        axis=0,
    )


def take_lanes(table, lanes):
    return jnp.take_along_axis(table, lanes, axis=1, mode="promise_in_bounds")


def inverse_sym(matrix):
    cofactor = [
        matrix[3] * matrix[5] - matrix[4] * matrix[4],
        matrix[2] * matrix[4] - matrix[1] * matrix[5],
        matrix[1] * matrix[4] - matrix[2] * matrix[3],
        matrix[0] * matrix[5] - matrix[2] * matrix[2],
        matrix[1] * matrix[2] - matrix[0] * matrix[4],
        matrix[0] * matrix[3] - matrix[1] * matrix[1],
    ]
    determinant = matrix[0] * cofactor[0] + matrix[1] * cofactor[1] + matrix[2] * cofactor[2]
    return [cofactor_entry / determinant for cofactor_entry in cofactor]


def apply_sym(inverse, comp_one, comp_two, comp_three):
    return [
        inverse[0] * comp_one + inverse[1] * comp_two + inverse[2] * comp_three,
        inverse[1] * comp_one + inverse[3] * comp_two + inverse[4] * comp_three,
        inverse[2] * comp_one + inverse[4] * comp_two + inverse[5] * comp_three,
    ]


def pack_kernel(
    num_hbm,
    den_hbm,
    bias_hbm,
    chain_hbm,
    list_hbm,
    counts_hbm,
    obs_hbm,
    prior_hbm,
    pick_hbm,
    point_hbm,
    out_ref,
    num_ref,
    den_ref,
    bias_ref,
    chain_ref,
    list_ref,
    counts_ref,
    obs_ref,
    prior_ref,
    pick_ref,
    point_ref,
    table_ref,
    sems,
):
    copies = [
        pltpu.make_async_copy(source, target, sems.at[index])
        for index, (source, target) in enumerate(
            [
                (num_hbm, num_ref),
                (den_hbm, den_ref),
                (bias_hbm, bias_ref),
                (chain_hbm, chain_ref),
                (list_hbm, list_ref),
                (counts_hbm, counts_ref),
                (obs_hbm, obs_ref),
                (prior_hbm, prior_ref),
                (pick_hbm, pick_ref),
                (point_hbm, point_ref),
            ]
        )
    ]
    for copy in copies:
        copy.start()
    owners = out_ref.shape[0] // BUCKET_ROWS
    scenes = num_ref.shape[1]
    listed = list_ref.shape[1]
    table_ref[...] = jnp.zeros(table_ref.shape, F32)
    for copy in copies[:5]:
        copy.wait()
    numer = num_ref[...].astype(F32)
    denom = den_ref[...].astype(F32)
    for which in range(2):
        table_ref[16 * which : 16 * which + 16, :] = numer[20 * which : 20 * which + 16]
        table_ref[33 + 16 * which : 48 + 16 * which, :] = denom[19 * which : 19 * which + 15]
        late = LATE_TERMS + 4 * which
        table_ref[late : late + 4, :] = numer[20 * which + 16 : 20 * which + 20]
        table_ref[late + 8 : late + 12, :] = denom[19 * which + 15 : 19 * which + 19]
    for part, value in enumerate(split3(bias_ref[...])):
        first = BIAS_ROW + part * SUB
        table_ref[first : first + 6, :] = value
    place = (chain_ref[...] & (scenes - 1)) + (lane_iota((1, scenes)) // (scenes // 4)) * scenes
    table_ref[CHAIN_ROW : CHAIN_ROW + 1, :] = (place >> 8).astype(F32)
    table_ref[CHAIN_ROW + 1 : CHAIN_ROW + 2, :] = (place & 255).astype(F32)
    table = table_ref[...].astype(BF16)
    lane = lane_iota((SUB, LANES))
    per_row = LANES // SUB
    index = (lane % per_row) * SUB + sublane_iota((SUB, LANES))
    lists = jnp.zeros((SUB, LANES), F32)
    for row in range(listed // LANES):
        ids = list_ref[:, row * LANES : (row + 1) * LANES].astype(F32)
        found = take_lanes(jnp.broadcast_to(ids, (SUB, LANES)), index)
        lists = jnp.where(lane // per_row == row, found, lists)
    lows = []
    for first in range(0, scenes, 256):
        inside = (lists >= float(first)) & (lists < float(first + 256))
        lows.append(jnp.where(inside, lists - float(first), -1.0))
    got = []
    for pair in range(0, SUB, 2):
        onehot = []
        for k in (pair, pair + 1):
            onehot.append(
                jnp.concatenate([one_hot_rows(low[k : k + 1]) for low in lows], axis=0)
            )
        both = jnp.dot(
            table, jnp.concatenate(onehot, axis=1), preferred_element_type=F32
        )
        for part in range(0, 256, LANES):
            one = both[:, part : part + LANES]
            bias_rows = (
                one[BIAS_ROW : BIAS_ROW + SUB]
                + one[BIAS_ROW + SUB : BIAS_ROW + 2 * SUB]
                + one[BIAS_ROW + 2 * SUB : BIAS_ROW + 3 * SUB]
            )
            got.append(jnp.concatenate([one[:BIAS_ROW], bias_rows, one[CHAIN_ROW:]], axis=0))
    for block in range(SCENE_ROWS):
        words = slice(block * SCENE_LANES, (block + 1) * SCENE_LANES)
        turned = jnp.concatenate([one[words] for one in got], axis=0).T
        for group in range(owners // SUB):
            out_ref[
                pl.ds(group * SUB * BUCKET_ROWS + 8 + block, SUB, stride=BUCKET_ROWS), :
            ] = turned[group * SUB : (group + 1) * SUB]
    for copy in copies[5:]:
        copy.wait()
    counts = jnp.broadcast_to(counts_ref[...].astype(F32), (owners, owners)).T
    slot = lane.astype(F32)
    for group in range(owners // SUB):
        live_count = counts[group * SUB : (group + 1) * SUB, :1]
        base = group * SUB * BUCKET_ROWS

        def put(row, value):
            out_ref[pl.ds(base + row, SUB, stride=BUCKET_ROWS), :] = value

        for row in range(4):
            put(row, obs_ref[pl.ds(group * SUB * 4 + row, SUB, stride=4), :])
        for half in range(2):
            rows = pl.ds(group * SUB * 2 + half, SUB, stride=2)
            live = slot + float(half * LANES) < live_count
            put(4 + half, jnp.where(live, prior_ref[rows, :], 0.0))
            put(6 + half, (pick_ref[rows, :] * 2048 + point_ref[rows, :]).astype(F32))


def ratios(coef, east, north, up):
    east_sq, north_sq, up_sq = east * east, north * north, up * up
    east_north, east_up, north_up = east * north, east * up, north * up
    terms = [
        (1, None, None, None),
        (east, 1, None, None),
        (north, None, 1, None),
        (up, None, None, 1),
        (east_north, north, east, None),
        (east_up, up, None, east),
        (north_up, None, up, north),
        (east_sq, 2.0 * east, None, None),
        (north_sq, None, 2.0 * north, None),
        (up_sq, None, None, 2.0 * up),
        (east_north * up, north_up, east_up, east_north),
        (east_sq * east, 3.0 * east_sq, None, None),
        (east * north_sq, north_sq, 2.0 * east_north, None),
        (east * up_sq, up_sq, None, 2.0 * east_up),
        (east_sq * north, 2.0 * east_north, east_sq, None),
        (north_sq * north, None, 3.0 * north_sq, None),
        (north * up_sq, None, up_sq, 2.0 * north_up),
        (east_sq * up, 2.0 * east_up, None, east_sq),
        (north_sq * up, None, 2.0 * north_up, north_sq),
        (up_sq * up, None, None, 3.0 * up_sq),
    ]
    sums = [[None] * 4 for _ in range(4)]
    for cubic in (2, 3):
        sums[cubic][0] = jnp.ones_like(east)

    def add(cubic, term, row):
        if cubic >= 2 and term == 0:
            return
        value = coef(row)
        for which, factor in enumerate(terms[term]):
            if factor is None:
                continue
            product = value if isinstance(factor, int) else value * factor
            held = sums[cubic][which]
            sums[cubic][which] = product if held is None else held + product

    words = [w for first in range(LANE_STEP) for w in range(first, SCENE_LANES, LANE_STEP)]
    bias = [None] * 6
    for word in words:
        for cubic in range(4):
            add(cubic, word, cubic * SCENE_LANES + word)
        add(word // 4, 16 + word % 4, LATE_TERMS + word)
        if word < 6:
            bias[word] = coef(BIAS_ROW + word)
    found = []
    for top, bottom in ((sums[0], sums[2]), (sums[1], sums[3])):
        quotient = top[0] / bottom[0]
        found.append(quotient)
        found.append(
            [(top[which] - quotient * bottom[which]) / bottom[0] for which in range(1, 4)]
        )
    return found, bias


def tile_kernel(
    got_ref,
    ground_ref,
    next_ref,
    out_ref,
    packed_ref,
    parts_ref,
    sums_ref,
    table_ref,
    step_ref,
    total_ref,
    place_ref,
    halo_ref,
    coef_ref,
    terms_ref,
    scene_ref,
    *,
    strips,
):
    owners = got_ref.shape[0] // BUCKET_ROWS
    groups = owners // SUB
    tiles = owners // strips
    points = ground_ref.shape[1]
    point_rows = points // LANES
    vreg = (SUB, LANES)
    lane = lane_iota(vreg)

    def fill_table(value):
        for axis in range(3):
            for row in range(point_rows):
                at = (axis * point_rows + row) * SUB
                table_ref[at : at + SUB, :] = jnp.broadcast_to(value(axis, row), vreg)

    fill_table(lambda axis, row: ground_ref[axis : axis + 1, row * LANES : (row + 1) * LANES])

    def tie_row(group, row):
        return got_ref[pl.ds(group * (SUB * BUCKET_ROWS) + row, SUB, stride=BUCKET_ROWS), :]

    def code_of(group, half):
        code = tie_row(group, 6 + half).astype(I32)
        return code >> 11, code & (points - 1)

    def gather_points(point):
        high = point >> 7
        low = point & (LANES - 1)
        bits = [(high & (1 << bit)) != 0 for bit in range((point_rows - 1).bit_length())]

        def pick(axis, first, bit):
            if bit < 0:
                at = (axis * point_rows + first) * SUB
                return take_lanes(table_ref[at : at + SUB, :], low)
            return jnp.where(
                bits[bit], pick(axis, first + (1 << bit), bit - 1), pick(axis, first, bit - 1)
            )

        found = [pick(axis, 0, len(bits) - 1) for axis in range(3)]
        return found

    def turn_scenes(group):
        for block in range(SCENE_ROWS):
            value = tie_row(group, 8 + block)
            for word in range(0, SCENE_LANES if block < 5 else 6, LANE_STEP):
                at = (block * SCENE_LANES + word) * SUB
                coef_ref[group % BUFFERS, at : at + SUB, :] = (
                    pltpu.roll(value, LANES - word, 1) if word else value
                )

    def first_pass(group, half):
        pick, point = code_of(group, half)
        first_lane = pick * SCENE_LANES
        east, north, up = gather_points(point)

        def coef(row):
            at = (row - row % LANE_STEP) * SUB
            return take_lanes(
                coef_ref[group % BUFFERS, at : at + SUB, :], first_lane + row % LANE_STEP
            )

        line_obs = tie_row(group, 2 * half)
        samp_obs = tie_row(group, 2 * half + 1)
        prior = tie_row(group, 4 + half)
        (line_ratio, line_jac, samp_ratio, samp_jac), bias = ratios(coef, east, north, up)
        line_res = line_obs - (line_ratio + bias[0] + bias[1] * samp_obs + bias[2] * line_obs)
        samp_res = samp_obs - (samp_ratio + bias[3] + bias[4] * samp_obs + bias[5] * line_obs)
        weight = prior / (1.0 + (line_res * line_res + samp_res * samp_res) / cauchy_scale)
        place = pl.ds((group * 2 + half) * SUB, SUB)
        for row, value in enumerate([line_res, samp_res] + line_jac + samp_jac + [weight]):
            packed_ref[row, place, :] = value
        pairs = [(0, 0), (0, 1), (0, 2), (1, 1), (1, 2), (2, 2)]
        sums = [weight * (line_jac[a] * line_jac[b] + samp_jac[a] * samp_jac[b]) for a, b in pairs]
        sums += [weight * (line_jac[a] * line_res + samp_jac[a] * samp_res) for a in range(3)]

        def put(row, value):
            parts_ref[
                group % BUFFERS, pl.ds(half * PART_ROWS + row, SUB, stride=BUCKET_PARTS), :
            ] = value

        for row, value in enumerate(sums):
            for part, piece in enumerate(split3(value)):
                put(row * 3 + part, piece)
        put(27, (point >> 8).astype(F32))
        put(28, (point & 255).astype(F32))

    wide = (16, LANES)
    steps_iota = [
        (sublane_iota(wide) + 16 * row).astype(F32).astype(BF16) for row in range(16)
    ]
    one = jnp.ones(wide, BF16)
    zero = jnp.zeros(wide, BF16)

    def product_of(group, first_bucket, count):
        held = parts_ref.at[group % BUFFERS]
        left = []
        right = []
        for bucket in range(first_bucket, first_bucket + count):
            for half in range(2):
                first = bucket * BUCKET_PARTS + half * PART_ROWS
                values = held[first : first + PART_ROWS, :].astype(BF16)
                high = jnp.broadcast_to(held[first + 27 : first + 28, :], wide).astype(BF16)
                low = jnp.broadcast_to(held[first + 28 : first + 29, :], wide).astype(BF16)
                rows = []
                for index in range(8):
                    here = high == jnp.full(wide, index, BF16)
                    rows.append(jnp.where(here, values[:16], zero))
                    rows.append(jnp.where(here, values[16:], zero))
                left.append(jnp.concatenate(rows, axis=0))
                right.append(
                    jnp.concatenate(
                        [jnp.where(low == step, one, zero) for step in steps_iota], axis=0
                    )
                )
        return lax.dot_general(
            jnp.concatenate(left, axis=1),
            jnp.concatenate(right, axis=1),
            (((1,), (1,)), ((), ())),
            preferred_element_type=F32,
        )

    def sum_pass(group, first_bucket, count):
        products = [
            product_of(group, first_bucket + part * count // 2, count // 2)
            for part in range(2)
        ]
        product = products[0] + products[1]
        for half in range(2):
            for index in range(SUB):
                held = slice(index * SUM_ROWS, index * SUM_ROWS + PART_ROWS)
                rows = slice(index * PART_ROWS, (index + 1) * PART_ROWS)
                sums_ref[half, held, :] += product[rows, half * LANES : (half + 1) * LANES]

    sums_ref[...] = jnp.zeros(sums_ref.shape, F32)
    for group in range(groups + 1):
        if group < groups:
            turn_scenes(group)
        if group:
            sum_pass(group - 1, 0, SUB)
        if group < groups:
            for half in range(2):
                first_pass(group, half)

    def point_sum(row, half):
        return sum(
            sums_ref[half, pl.ds(row * 3 + part, SUB, stride=SUM_ROWS), :] for part in (2, 1, 0)
        )

    for half in range(2):
        sums = [point_sum(row, half) for row in range(9)]
        matrix = [
            sums[0] + point_damping,
            sums[1],
            sums[2],
            sums[3] + point_damping,
            sums[4],
            sums[5] + point_damping,
        ]
        steps = apply_sym(inverse_sym(matrix), sums[6], sums[7], sums[8])
        for axis in range(3):
            step_ref[pl.ds(axis * point_rows + half, SUB, stride=2), :] = steps[axis]
    for axis in range(3):
        for row in range(point_rows):
            columns = slice(row * LANES, (row + 1) * LANES)
            at = axis * point_rows + row
            next_ref[axis : axis + 1, columns] = (
                ground_ref[axis : axis + 1, columns] + step_ref[at : at + 1, :]
            )
    fill_table(
        lambda axis, row: step_ref[axis * point_rows + row : axis * point_rows + row + 1, :]
    )

    def tie_terms(group, slot):
        rows = []
        picks = []
        for half in range(2):
            pick, point = code_of(group, half)
            tie_step = gather_points(point)
            place = pl.ds((group * 2 + half) * SUB, SUB)
            packed = [packed_ref[row, place, :] for row in range(9)]
            line_obs = tie_row(group, 2 * half)
            samp_obs = tie_row(group, 2 * half + 1)
            weight = packed[8]
            line_res = packed[0] - (
                packed[2] * tie_step[0] + packed[3] * tie_step[1] + packed[4] * tie_step[2]
            )
            samp_res = packed[1] - (
                packed[5] * tie_step[0] + packed[6] * tie_step[1] + packed[7] * tie_step[2]
            )
            samp_weight = weight * samp_obs
            line_weight = weight * line_obs
            rows.append(
                [
                    weight,
                    samp_weight,
                    line_weight,
                    samp_weight * samp_obs,
                    samp_weight * line_obs,
                    line_weight * line_obs,
                    weight * line_res,
                    samp_weight * line_res,
                    line_weight * line_res,
                    weight * samp_res,
                    samp_weight * samp_res,
                    line_weight * samp_res,
                ]
            )
            picks.append(pick)
        for half in range(2):
            spare = [jnp.zeros(vreg, F32)] * 3
            for row, value in enumerate(rows[half] + [picks[half].astype(F32)] + spare):
                terms_ref[slot * 2 + half, pl.ds(row, SUB, stride=TERM_ROWS), :] = value

    def scene_sums(group, slot):
        for bucket in range(SUB):
            chosen = []
            pieces = [[], [], []]
            for half in range(2):
                first = bucket * TERM_ROWS
                pick = jnp.broadcast_to(
                    terms_ref[slot * 2 + half, first + 12 : first + 13, :], wide
                ).astype(BF16)
                chosen.append(jnp.where(pick == steps_iota[0], one, zero))
                for part, piece in enumerate(split3(terms_ref[slot * 2 + half, first : first + 16, :])):
                    pieces[part].append(piece.astype(BF16))
            scene_ref[slot, bucket * SUB : (bucket + 1) * SUB, :SCENE_LANES] = lax.dot_general(
                jnp.concatenate(chosen * 3, axis=1),
                jnp.concatenate(pieces[0] + pieces[1] + pieces[2], axis=1),
                (((1,), (1,)), ((), ())),
                preferred_element_type=F32,
            )[:SUB]
        total = scene_ref[slot, pl.ds(0, SUB, stride=SUB), :]
        for scene in range(1, 8):
            value = pltpu.roll(
                scene_ref[slot, pl.ds(scene, SUB, stride=SUB), :], scene * SCENE_LANES, 1
            )
            total = jnp.where(lane // SCENE_LANES == scene, value, total)
        place = pl.ds(group * SUB, SUB)
        total_ref[place, :] = total
        chain = tie_row(group, 8 + CHAIN_SENT // SCENE_LANES)
        chain_lane = (lane // SCENE_LANES) * SCENE_LANES + CHAIN_SENT % SCENE_LANES
        place_ref[place, :] = take_lanes(chain, chain_lane) * 256.0 + take_lanes(
            chain, chain_lane + 1
        )

    def second_pass(step, carry):
        for slot in range(TOGETHER):
            tie_terms(step * TOGETHER + slot, slot)
        for slot in range(TOGETHER):
            scene_sums(step * TOGETHER + slot, slot)
        return carry

    lax.fori_loop(0, groups // TOGETHER, second_pass, 0)

    segment = 4 * LANES
    word = lane % SCENE_LANES
    stacked = []
    for near in range(HALO):
        rows = []
        for strip in range(strips):
            for side in range(2):
                at = float(strip * segment + (near if side else segment - HALO + near))
                for block in range(0, tiles, SUB):
                    here = [pl.ds(s * tiles + block, SUB) for s in range(strips)]
                    rows.append(
                        sum(jnp.where(place_ref[h, :] == at, total_ref[h, :], 0.0) for h in here)
                    )
        stacked.append(jnp.concatenate(rows, axis=0))
    stacked = jnp.concatenate(stacked, axis=1)
    source = sublane_iota((HALO * LANES, 2 * LANES))
    target = lane_iota((HALO * LANES, 2 * LANES))
    chosen = (source % SCENE_LANES == target // SCENE_LANES) & (
        target % SCENE_LANES == source // LANES + POS_LANE + 1
    )
    chosen = jnp.where(chosen, 1.0, 0.0).astype(BF16)
    moved = sum(
        jnp.dot(part.astype(BF16), chosen, preferred_element_type=F32)
        for part in reversed(split3(stacked))
    )
    flag = lane // SCENE_LANES == 4
    for side in range(2):
        for part in range(2):
            for strip in range(strips):
                slot = strip * 4 + side * 2 + part
                edge = tiles if side else SUB
                halo_ref[slot, edge : edge + SUB, :] = jnp.zeros(vreg, F32)
                for block in range(0, tiles, SUB):
                    at = (strip * 2 + side) * tiles + block
                    value = moved[at : at + SUB, part * LANES : (part + 1) * LANES]
                    if part:
                        value = jnp.where(flag, 1.0, value)
                    first = SUB + block + (-1 if side else 1)
                    halo_ref[slot, first : first + SUB, :] = value
    for strip in range(strips):
        start = float(strip * segment)
        for block in range(0, tiles, SUB):
            for source in range(strips):
                place = place_ref[pl.ds(source * tiles + block, SUB), :] - start
                inside = (place >= 0.0) & (place < float(segment))
                value = total_ref[pl.ds(source * tiles + block, SUB), :]
                value = jnp.where(word == POS_LANE, jnp.where(inside, place, -1.0), value)
                value = jnp.where(
                    word > POS_LANE,
                    halo_ref[strip * 4 + source, SUB + block : 2 * SUB + block, :],
                    value,
                )
                out_ref[
                    pl.ds((strip * tiles + block) * strips + source, SUB, stride=strips), :
                ] = value


def chain_kernel(got_ref, out_ref, turned_ref, joined_ref, *, coupling):
    scenes = out_ref.shape[1]
    parts = scenes // 256
    part_rows = 3 * SCENE_LANES
    total = jnp.zeros((parts * part_rows, 256), F32)
    border = jnp.zeros((SUB, LANES), F32)
    for first in range(0, got_ref.shape[0], LANES):
        block = got_ref[first : first + LANES, :]
        for row in range(0, LANES, SUB):
            border = border + block[row : row + SUB]
        turned = block.T
        values = jnp.concatenate(
            [turned[k * SCENE_LANES : (k + 1) * SCENE_LANES] for k in range(8)], axis=1
        )
        position = values[POS_LANE : POS_LANE + 1]
        part_of = (position * (1.0 / 256.0)).astype(I32).astype(F32)
        held = jnp.broadcast_to(part_of, values.shape).astype(BF16)
        pieces = [piece.astype(BF16) for piece in split3(values)]
        zero = jnp.zeros(values.shape, BF16)
        left = [
            jnp.where(held == jnp.full(values.shape, part, BF16), piece, zero)
            for part in range(parts)
            for piece in pieces
        ]
        total = total + lax.dot_general(
            jnp.concatenate(left, axis=0),
            one_hot_rows(position - 256.0 * part_of),
            (((1,), (1,)), ((), ())),
            preferred_element_type=F32,
        )
    sums = jnp.concatenate(
        [
            total[first + 32 : first + 48] + total[first + 16 : first + 32] + total[first : first + 16]
            for first in range(0, parts * part_rows, part_rows)
        ],
        axis=1,
    )
    sums = jnp.where(sublane_iota(sums.shape) == POS_LANE, 1.0, sums)

    border = border + pltpu.roll(border, 4, 0)
    turned_ref[...] = jnp.concatenate([border] * (LANES // SUB), axis=0).T
    lane = lane_iota((SUB, LANES))
    sides = []
    for side in range(2):
        parts = []
        for part in range(2):
            value = jnp.zeros((SUB, LANES), F32)
            for near in range(HALO):
                column = turned_ref[pl.ds(POS_LANE + 1 + near, SUB, stride=SCENE_LANES), :]
                row = side * 2 + part
                here = lane == (near if side else LANES - HALO + near)
                value = jnp.where(here, column[:, row : row + 1], value)
            parts.append(value)
        sides.append(jnp.concatenate(parts, axis=0))
    sums = jnp.concatenate([sides[0], sums, sides[1]], axis=1)
    width = sums.shape[1]
    joined_ref[...] = sums
    rows = [joined_ref[row : row + 1, :] for row in range(6)]
    matrix = [
        rows[0] + 2.0 * coupling,
        rows[1],
        rows[2],
        rows[3] + 2.0 * coupling,
        rows[4],
        rows[5] + 2.0 * coupling,
    ]
    exists = joined_ref[POS_LANE : POS_LANE + 1, :] > 0.0
    inverse = [
        jnp.broadcast_to(jnp.where(exists, entry, 0.0), (2, width))
        for entry in inverse_sym(matrix)
    ]
    right_sides = [
        jnp.concatenate(
            [joined_ref[6 + term : 7 + term, :], joined_ref[9 + term : 10 + term, :]], axis=0
        )
        for term in range(3)
    ]
    smoothed = apply_sym(inverse, *right_sides)
    for _ in range(SWEEPS - 1):
        smoothed = apply_sym(
            inverse,
            *[
                side + coupling * (pltpu.roll(value, 1, 1) + pltpu.roll(value, width - 1, 1))
                for side, value in zip(right_sides, smoothed)
            ],
        )
    for term in range(3):
        for row in range(2):
            out_ref[3 * row + term : 3 * row + term + 1, :] = smoothed[term][
                row : row + 1, LANES : LANES + scenes
            ]


def call(kernel, out_shape, scratch=(), name=None, vmem=48, **specs):
    return pl.pallas_call(
        kernel,
        out_shape=out_shape,
        scratch_shapes=list(scratch),
        compiler_params=pltpu.CompilerParams(vmem_limit_bytes=vmem * 1024 * 1024),
        name=name,
        **specs,
    )


def shape(dims, dtype=F32):
    return jax.ShapeDtypeStruct(dims, dtype)


def tile_call(got, ground, strips):
    owners = got.shape[0] // BUCKET_ROWS
    tie_rows = owners * 2
    points = ground.shape[1]
    return call(
        functools.partial(tile_kernel, strips=strips),
        (shape(ground.shape), shape((owners * strips, LANES))),
        [
            pltpu.VMEM((9, tie_rows, LANES), F32),
            pltpu.VMEM((BUFFERS, SUB * BUCKET_PARTS, LANES), F32),
            pltpu.VMEM((2, SUB * SUM_ROWS, LANES), F32),
            pltpu.VMEM((3 * points // LANES * SUB, LANES), F32),
            pltpu.VMEM((3 * points // LANES, LANES), F32),
            pltpu.VMEM((owners, LANES), F32),
            pltpu.VMEM((owners, LANES), F32),
            pltpu.VMEM((strips * 4, owners // strips + 2 * SUB, LANES), F32),
            pltpu.VMEM((BUFFERS, SCENE_ROWS * SCENE_LANES * SUB, LANES), F32),
            pltpu.VMEM((2 * TOGETHER, SUB * TERM_ROWS, LANES), F32),
            pltpu.VMEM((TOGETHER, SUB * SUB, LANES), F32),
        ],
        name="tile_sums",
    )(got, ground)


def per_device(
    num_coef,
    den_coef,
    bias,
    scene_chain,
    bucket_scenes,
    tie_counts,
    tie_obs,
    tie_prior,
    tie_pick,
    tie_point,
    ground,
):
    strips = lax.axis_size("strip")
    tiles = lax.axis_size("tile")
    owners = strips * tiles
    tie_dev = tie_prior.shape[0]
    tie_rows = tie_dev // LANES
    scenes_dev = num_coef.shape[1]
    coupling = smooth_gain * (tie_dev // scenes_dev)

    arguments = [
        num_coef,
        den_coef,
        bias,
        scene_chain.reshape(1, scenes_dev),
        bucket_scenes,
        tie_counts,
        tie_obs.reshape(2, tie_rows, LANES).transpose(1, 0, 2).reshape(2 * tie_rows, LANES),
        tie_prior.reshape(tie_rows, LANES),
        tie_pick.reshape(tie_rows, LANES),
        tie_point.reshape(tie_rows, LANES),
    ]
    sent = call(
        pack_kernel,
        shape((owners * BUCKET_ROWS, LANES)),
        [pltpu.VMEM(argument.shape, argument.dtype) for argument in arguments]
        + [
            pltpu.VMEM((CHAIN_ROW + SUB, scenes_dev), F32),
            pltpu.SemaphoreType.DMA((len(arguments),)),
        ],
        name="pack",
        vmem=64,
        in_specs=[pl.BlockSpec(memory_space=pltpu.HBM)] * len(arguments),
    )(*arguments)
    got = lax.all_to_all(
        sent.reshape(owners, BUCKET_ROWS // 2, 2, LANES), AXES, 0, 0, tiled=True
    ).reshape(owners * BUCKET_ROWS, LANES)
    ground_next, totals = tile_call(got, ground, strips)
    got_totals = lax.all_to_all(totals.reshape(owners, strips, LANES), AXES, 0, 0, tiled=True)
    smoothed = call(
        functools.partial(chain_kernel, coupling=coupling),
        shape((6, scenes_dev)),
        [pltpu.VMEM((LANES, LANES), F32), pltpu.VMEM((16, scenes_dev + 2 * LANES), F32)],
        name="chain",
    )(got_totals.reshape(owners * strips, LANES))
    return ground_next, smoothed


def solution(mesh):
    in_specs = (
        P(None, AXES),
        P(None, AXES),
        P(None, AXES),
        P(AXES),
        P(AXES, None),
        P(AXES, None),
        P(None, AXES),
        P(AXES),
        P(AXES),
        P(AXES),
        P(None, AXES),
    )
    out_specs = (P(None, AXES), P(None, AXES))
    return jax.shard_map(
        per_device, mesh=mesh, in_specs=in_specs, out_specs=out_specs, check_vma=False
    )
```
